256 devices in a mesh: wide: 32 (over y, z), narrow: 8 (over x, core).
Axes of the slice: x: 4, y: 4, z: 8, core: 2. Of those that a mesh axis runs over, the one named last changes fastest.
Arguments:
- entry_factor: bfloat16 [1152, 8, 64, 1024], P('wide', 'narrow'), may hold values from -6 to 6
- entry_panel: int32 [1152, 8], P('wide', 'narrow'), may hold values from 0 to 1
- entry_target: int32 [1152, 8], P('wide', 'narrow'), may hold values from 0 to 7, as said below
- entry_count: int32 [8, 32], P('narrow', 'wide'), may hold values from 1 to 36, 384 in all within a row
- panel_shared: bfloat16 [64, 64, 1024], P('wide', None, 'narrow'), may hold values from -0.1875 to 0.1875
- coupling: float32 [64, 64, 64], P('wide'), may hold values from -0.75 to 0.75
- probes: bfloat16 [64, 64, 1024], P('narrow'), may hold values from -6 to 6
Outputs:
- left_factor: float32 [64, 64, 1024], P('narrow', None, 'wide')
- right_factor: float32 [64, 64, 1024], P('narrow', None, 'wide')
The draws below stay inside these ranges and needn't reach their ends.
Inputs may be any that keep to these rules, and one draw needn't show every extreme that they name: `entry_panel`: the local panel of an entry of any slot, live or not. `entry_target`: the local target of an entry; every target has at least one live entry. `entry_count`: the live slots of one device; for every owner the counts over the 32 wide indices sum to 384, and some device holds exactly 36.
All inputs are finite; a program needn't handle non-finite values.
Results may differ from the reference program's by a relative error of at most 0.0036.
Values may be sent and summed in bfloat16 or wider, within the bound.
No kernel may reach another device: no remote copies, remote signals or barrier semaphores. Data moves between devices by JAX's collectives and lax.ppermute only.
A program may use at most 64 MiB of HBM per device.

```python
import math
import jax
import jax.numpy as jnp
import numpy as np
from jax import lax

B = 1024
R = 64
TGT_DEV = 8
DESC_DEV = 2
ENT_MEAN = 12
LIST_DEV = 36
OWNERS = 8
GROUPS = 32
TGT = 64
PANELS = 64
ENTRIES = 1152
N_WIDE = 32


def draw_entry_target(key, part):
    row_index = jnp.arange(ENTRIES, dtype=jnp.int32)[:, None]
    owner_index = jnp.arange(OWNERS, dtype=jnp.int32)[None, :]
    random_target = jax.random.randint(key, (ENTRIES, OWNERS), 0, TGT_DEV, dtype=jnp.int32)
    first_target = (row_index // LIST_DEV + owner_index) % TGT_DEV
    return jnp.where(row_index % LIST_DEV == 0, first_target, random_target).astype(jnp.int32)


def touch_ends(drawn, rng, least, high):
    shape = drawn.shape
    index_at = [jax.random.randint(jax.random.fold_in(rng, axis), (), 0, shape[axis]) for axis in range(len(shape))]
    drawn = drawn.at[tuple(index_at)].set(least)
    longest = shape.index(max(shape))
    index_at[longest] = (index_at[longest] + 1) % shape[longest]
    return drawn.at[tuple(index_at)].set(high)


def steps_of(own_key, shape, cuts, least, largest):
    level = 1.0
    for axis_at, blocks in cuts:
        draws = jax.random.uniform(jax.random.fold_in(jax.random.fold_in(own_key, 6), axis_at), (blocks,), jnp.float32, least / len(cuts), largest / len(cuts))
        level = level * jnp.repeat(jnp.exp(draws), shape[axis_at] // blocks).reshape((-1,) + (1,) * (len(shape) - 1 - axis_at))
    return level


def length_profile(count, total, bound, lean):
    loads = [(1 << 20) // math.isqrt(standing ** lean) + 1 for standing in range(2, count + 1)]
    rest, given = total - bound - (count - 1), [1] * (count - 1)
    while rest > 0:
        free = [i for i in range(count - 1) if given[i] < bound]
        whole, left = sum([loads[i] for i in free]), rest
        for i in free:
            addition = min(bound - given[i], max(1, left * loads[i] // whole), rest)
            given[i] = given[i] + addition
            rest = rest - addition
    return np.array([bound] + given)


def ragged_sizes(own_key, number_of, total, bound, lean):
    if number_of == 2:
        one = jax.random.randint(own_key, (), max(1, total - bound), min(bound, total - 1) + 1)
        return jnp.stack([one, total - one])
    tallies = jnp.asarray(length_profile(number_of, total, bound, lean), jnp.int32)
    pairs = (number_of - 1) // 2
    giver, taker = tallies[1:1 + 2 * pairs:2], tallies[2:2 + 2 * pairs:2]
    margin = jnp.minimum(giver - 1, bound - taker)
    moved = jax.random.randint(jax.random.fold_in(own_key, 1), (pairs,), 0, 1 << 20) % (margin + 1)
    tallies = tallies.at[1:1 + 2 * pairs:2].set(giver - moved).at[2:2 + 2 * pairs:2].set(taker + moved)
    return tallies[jax.random.permutation(jax.random.fold_in(own_key, 2), number_of)]


def centred(stream_key, extent, scale, reach, shards=(), kind=jnp.bfloat16):
    array = jax.random.normal(stream_key, extent, jnp.float32) * scale
    if len(shards) > 0:
        array = steps_of(stream_key, extent, shards, -0.22, 0.18) * array
    return jnp.clip(array, min=-reach, max=reach).astype(kind)


def setup_inputs(seed: int = 0) -> dict:
    seeds = jax.random.split(jax.random.key(seed), 8)
    return {
        "entry_factor": centred(seeds[0], (ENTRIES, OWNERS, R, B), 1.0, 6.0, ((0, 32), (1, 8))),
        "entry_panel": touch_ends(jax.random.randint(seeds[1], (ENTRIES, OWNERS), 0, DESC_DEV), jax.random.fold_in(seeds[1], 1), 0, DESC_DEV - 1).astype(jnp.int32),
        "entry_target": draw_entry_target(jax.random.fold_in(seeds[7], 71), 0),
        "entry_count": jax.vmap(lambda own: ragged_sizes(own, GROUPS, ENT_MEAN * N_WIDE, LIST_DEV, 2))(jax.random.split(seeds[3], OWNERS)).reshape((OWNERS, GROUPS)).astype(jnp.int32),
        "panel_shared": centred(seeds[4], (PANELS, R, B), B ** -0.5, 0.1875, ((0, 32), (2, 8))),
        "coupling": centred(seeds[5], (PANELS, R, R), R ** -0.5, 0.75, ((0, 32),), jnp.float32),
        "probes": centred(seeds[6], (TGT, R, B), 1.0, 6.0, ((0, 8),)),
    }


def rounded(value):
    return lax.optimization_barrier(value.astype(jnp.bfloat16)).astype(jnp.float32)

def reference(entry_factor, entry_panel, entry_target, entry_count, panel_shared, coupling, probes):
    highest = lax.Precision.HIGHEST
    owner_count = entry_factor.shape[1]
    rank_dim = entry_factor.shape[2]
    full_width = entry_factor.shape[3]
    slot_ids = jnp.arange(LIST_DEV, dtype=jnp.int32)
    panel_ids = jnp.arange(DESC_DEV, dtype=jnp.int32)
    target_ids = jnp.arange(TGT_DEV, dtype=jnp.int32)
    probe_blocks = probes.astype(jnp.float32).reshape(owner_count, TGT_DEV, rank_dim, full_width)

    def group_data(group_index):
        entry_start = (group_index * LIST_DEV).astype(jnp.int32)
        factors = lax.dynamic_slice_in_dim(entry_factor, entry_start, LIST_DEV, 0).astype(jnp.float32)
        panels = lax.dynamic_slice_in_dim(entry_panel, entry_start, LIST_DEV, 0)
        targets = lax.dynamic_slice_in_dim(entry_target, entry_start, LIST_DEV, 0)
        counts = lax.dynamic_index_in_dim(entry_count, group_index, 1, keepdims=False)
        live_mask = (slot_ids[:, None] < counts[None, :]).astype(jnp.float32)
        pick_panel = (panels[:, :, None] == panel_ids[None, None, :]).astype(jnp.float32) * live_mask[:, :, None]
        pick_target = (targets[:, :, None] == target_ids[None, None, :]).astype(jnp.float32)
        panel_start = (group_index * DESC_DEV).astype(jnp.int32)
        shared = lax.dynamic_slice_in_dim(panel_shared, panel_start, DESC_DEV, 0).astype(jnp.float32)
        middle = lax.dynamic_slice_in_dim(coupling, panel_start, DESC_DEV, 0).astype(jnp.float32)
        return (factors, pick_panel, pick_target, shared, middle)

    def first_pass(sketch, group_index):
        factors, pick_panel, pick_target, shared, middle = group_data(group_index)
        projected = jnp.einsum('drb,otkb->dotrk', shared, probe_blocks, precision=highest)
        coefficients = rounded(jnp.einsum('dij,dotjk->dotik', middle, projected, precision=highest))
        weights = jnp.einsum('lod,lot->lodt', pick_panel, pick_target)
        chosen = jnp.einsum('lodt,dotik->loik', weights, coefficients, precision=highest)
        contributions = jnp.einsum('loji,lojb->loib', chosen, factors, precision=highest)
        return (sketch + jnp.einsum('lot,loib->otib', pick_target, contributions, precision=highest), None)
    zeros = jnp.zeros((owner_count, TGT_DEV, rank_dim, full_width), jnp.float32)
    group_list = jnp.arange(GROUPS, dtype=jnp.int32)
    sketch, _ = lax.scan(first_pass, zeros, group_list)
    gram_matrix = jnp.einsum('otib,otjb->otij', sketch, sketch, precision=highest)
    lower_factor = jnp.linalg.cholesky(gram_matrix)
    basis = lax.linalg.triangular_solve(lower_factor, sketch, left_side=True, lower=True)
    basis_round = rounded(basis)

    def second_pass(coeff_rows, group_index):
        factors, pick_panel, pick_target, shared, middle = group_data(group_index)
        selected = jnp.einsum('lot,otkb->lokb', pick_target, basis_round, precision=highest)
        back_terms = jnp.einsum('loib,lokb->loik', factors, selected, precision=highest)
        weights = jnp.einsum('lod,lot->lodt', pick_panel, pick_target)
        summed = jnp.einsum('lodt,loik->dotik', weights, back_terms, precision=highest)
        middle_terms = jnp.einsum('dotik,dij->dotkj', summed, middle, precision=highest)
        return (coeff_rows + jnp.einsum('dotkj,djb->otkb', middle_terms, shared, precision=highest), None)
    coeff_rows, _ = lax.scan(second_pass, zeros, group_list)
    root_width = math.sqrt(full_width)
    left_factor = (basis * root_width).reshape(TGT, rank_dim, full_width)
    right_factor = (coeff_rows / root_width).reshape(TGT, rank_dim, full_width)
    return (left_factor, right_factor)
```

```python
import functools
import math

import jax
import jax.numpy as jnp
from jax import lax
from jax.experimental import pallas as pl
from jax.experimental.pallas import tpu as pltpu
from jax.sharding import Mesh
from jax.sharding import PartitionSpec as P

BF = jnp.bfloat16
F32 = jnp.float32
HIGHEST = lax.Precision.HIGHEST
NT = (((1,), (1,)), ((), ()))
TN = (((0,), (0,)), ((), ()))
SMEM = pltpu.SMEM
VMEM = pltpu.VMEM
LANES = 128
TAIL = 16


def params(mib):
    return pltpu.CompilerParams(vmem_limit_bytes=mib * 1024 * 1024)


def split_bf(x, parts):
    out = []
    for _ in range(parts):
        part = x.astype(BF)
        out.append(part)
        x = x - part.astype(F32)
    return out


def pack_rows(block):
    return jnp.concatenate([block[q * TAIL : (q + 1) * TAIL] for q in range(block.shape[0] // TAIL)], axis=1)


def unpack_rows(ref, lead, row, first, count):
    return jnp.concatenate(
        [ref[lead, row : row + TAIL, q * LANES : (q + 1) * LANES] for q in range(first, first + count)], axis=0
    )


def sum_factors(panel, target, count, factors, out, acc):
    pairs = acc.shape[0]
    panels = pairs // 8
    rank = acc.shape[1]

    def clear(i, _):
        acc[i] = jnp.zeros(acc.shape[1:], F32)
        return 0

    lax.fori_loop(0, pairs, clear, 0)

    def add(e, _):
        pair = target[e] * panels + panel[e]
        acc[pair] += factors[e].astype(F32)
        return 0

    lax.fori_loop(0, count[0], add, 0)
    groups = out.shape[0]
    each = pairs // groups
    for i in range(pairs):
        row = (i % each) * rank
        out[i // each, row : row + rank, :] = acc[i].astype(BF)


def project(columns, *refs):
    pieces, (probes, coupling, _, sent, shared, tails, sem) = refs[:-7], refs[-7:]
    rows = pieces[0].shape[1]
    at = 0
    for piece in pieces:
        for half in range(piece.shape[0]):
            start = pl.multiple_of(columns[at] * LANES, LANES)
            shared[0:rows, pl.ds(start, LANES)] = piece[half]
            at += 1
    rank = coupling.shape[1]
    zero = jnp.zeros((rank, rank), F32)
    first, second = coupling[0], coupling[1]
    diagonal = jnp.concatenate(
        [jnp.concatenate([first, zero], axis=1), jnp.concatenate([zero, second], axis=1)], axis=0
    )
    projected = lax.dot_general(probes[...], shared[0:rows, :], NT, preferred_element_type=F32)
    coefficients = lax.dot_general(
        projected, diagonal, NT, precision=HIGHEST, preferred_element_type=F32
    ).astype(BF)
    groups = tails.shape[0]
    each = coefficients.shape[0] // groups
    for g in range(groups):
        part = coefficients[g * each : (g + 1) * each]
        tails[g, :, 0 : each * 8] = pack_rows(part)
    copy = pltpu.make_async_copy(tails, sent.at[:, sent.shape[1] - TAIL :, :], sem)
    copy.start()
    high, mid, low = split_bf(jnp.concatenate([first, second], axis=1), 3)
    shared[rows : rows + TAIL, :] = jnp.concatenate([pack_rows(high), pack_rows(mid)], axis=1)
    tail = pack_rows(low)
    shared[rows + TAIL : rows + 2 * TAIL, :] = jnp.concatenate([tail, jnp.zeros_like(tail)], axis=1)
    copy.wait()


def first_pass(held, out):
    groups, rows, width = held.shape
    rows = rows - TAIL
    targets = rows // LANES
    rank = out.shape[1] // targets
    cut = out.shape[2]
    for t in range(targets):
        total = jnp.zeros((rank, width), F32)
        for g in range(groups):
            coefficients = unpack_rows(held, g, rows, t * (rank // TAIL), rank // TAIL)
            total = total + jnp.dot(
                coefficients, held[g, t * LANES : (t + 1) * LANES, :], preferred_element_type=F32
            )
        for z in range(out.shape[0]):
            out[z, t * rank : (t + 1) * rank, :] = total[:, z * cut : (z + 1) * cut]


def add_up(parts, out):
    total = parts[0]
    for z in range(1, parts.shape[0]):
        total = total + parts[z]
    for z in range(out.shape[0]):
        out[z] = total


def inverse_factors(grams):
    rank = grams[0].shape[0]
    row_at = lax.broadcasted_iota(jnp.int32, (rank, 2 * rank), 0)
    lane_at = lax.broadcasted_iota(jnp.int32, (rank, 2 * rank), 1)
    eye = (row_at + rank == lane_at).astype(F32)
    tables = [jnp.concatenate([g, jnp.zeros((rank, rank), F32)], axis=1) + eye for g in grams]
    scales = [jnp.ones((rank, 2 * rank), F32) for _ in grams]
    for k in range(rank):
        for i, table in enumerate(tables):
            top = (k // 8) * 8
            pivot_row = table[k : k + 1, :]
            pivot = pivot_row[:, k : k + 1]
            scaled = pivot_row * (1.0 / pivot)
            column = table[top:, k : k + 1]
            below = row_at[top:, :] > k
            lower = table[top:, :] - jnp.where(below, column * scaled, 0.0)
            tables[i] = lower if top == 0 else jnp.concatenate([table[:top], lower], axis=0)
            scales[i] = jnp.where(row_at == k, pivot, scales[i])
    return [(table * lax.rsqrt(scale))[:, rank:] for table, scale in zip(tables, scales, strict=True)]


def orthonormal(place, sketches, rounded, *refs):
    left, (basis, turned) = refs[:-2], refs[-2:]
    groups, rows, cut = sketches.shape
    targets = 2
    rank = rows // targets
    own = left[0].shape[0]
    owners = len(left)
    width = groups * cut
    whole = [
        jnp.concatenate([sketches[z, t * rank : (t + 1) * rank, :] for z in range(groups)], axis=1)
        for t in range(targets)
    ]
    grams = [lax.dot_general(s, s, NT, precision=HIGHEST, preferred_element_type=F32) for s in whole]
    inverses = inverse_factors(grams)
    for t in range(targets):
        found = jnp.dot(inverses[t], whole[t], precision=HIGHEST, preferred_element_type=F32)
        basis[t * rank : (t + 1) * rank, :] = found
        rounded[t * rank : (t + 1) * rank, :] = found.astype(BF)
    for s in range(owners):
        owner = lax.rem(place[0] + s, owners)
        start = owner * (width // owners) + place[1] * own
        aligned = (start // LANES) * LANES
        turned[...] = basis[:, pl.ds(pl.multiple_of(aligned, LANES), LANES)].T
        left[s][...] = turned[pl.ds(pl.multiple_of(start - aligned, 32), own), :]


def second_pass(held, rounded, shared, out):
    groups, rows, width = held.shape
    rows = rows - TAIL
    targets = rows // LANES
    rank = rounded.shape[0] // targets
    total = jnp.zeros((rounded.shape[0], width), F32)
    for g in range(groups):
        summed = jnp.concatenate(
            [
                lax.dot_general(
                    held[g, t * LANES : (t + 1) * LANES, :],
                    rounded[t * rank : (t + 1) * rank, :],
                    NT,
                    preferred_element_type=F32,
                )
                for t in range(targets)
            ],
            axis=1,
        )
        coupling = (
            unpack_rows(shared, g, LANES, 0, 4).astype(F32) + unpack_rows(shared, g, LANES, 4, 4).astype(F32)
        ) + unpack_rows(shared, g, LANES + TAIL, 0, 4).astype(F32)
        middle = jnp.concatenate(
            [
                lax.dot_general(
                    coupling[:, d * rank : (d + 1) * rank],
                    summed[d * rank : (d + 1) * rank, :],
                    TN,
                    precision=HIGHEST,
                    preferred_element_type=F32,
                )
                for d in range(LANES // rank)
            ],
            axis=0,
        ).T
        for part in split_bf(middle, 2):
            total = total + jnp.dot(part, shared[g, 0:LANES, :], preferred_element_type=F32)
    for c in range(width // LANES):
        out[c * LANES : (c + 1) * LANES, :] = total[:, c * LANES : (c + 1) * LANES].T.astype(out.dtype)


def finish(place, parts, *refs):
    left_parts, (left, right) = refs[:-2], refs[-2:]
    owners = len(left_parts)
    groups = parts.shape[0] // owners
    targets = left.shape[0] // owners
    rank = left.shape[2]
    root = math.sqrt(1024)
    for y in range(owners):
        total = parts[y * groups].astype(F32)
        for z in range(1, groups):
            total = total + parts[y * groups + z].astype(F32)
        total = total / root
        for t in range(targets):
            right[y * targets + t] = total[:, t * rank : (t + 1) * rank]
    for s in range(owners):
        owner = lax.rem(place[0] + owners - s, owners)
        rows = left_parts[s][...] * root
        for t in range(targets):
            left[owner * targets + t] = rows[:, t * rank : (t + 1) * rank]


def shards(sizes, entry_factor, entry_panel, entry_target, entry_count, panel_shared, coupling, probes):
    ny, nz, nx, nc = sizes
    y, z = lax.axis_index("y"), lax.axis_index("z")
    x, c = lax.axis_index("x"), lax.axis_index("core")
    place = jnp.stack([y, z]).astype(jnp.int32)
    factors = entry_factor[:, 0]
    slots, rank, width = factors.shape
    panels = panel_shared.shape[0]
    targets = probes.shape[0]
    rows = panels * rank
    mine = targets // ny
    held_rows = mine * panels * rank + TAIL
    in_vmem = pl.BlockSpec(memory_space=VMEM)
    in_smem = pl.BlockSpec(memory_space=SMEM)
    in_any = pl.BlockSpec(memory_space=pl.ANY)

    own = panel_shared.reshape(rows, LANES)
    other = lax.ppermute(own, "core", [(i, (i + 1) % nc) for i in range(nc)])
    pair = jnp.stack([own, other])
    pieces = [pair] + [lax.ppermute(pair, "x", [(i, (i + s) % nx) for i in range(nx)]) for s in range(1, nx)]
    columns = jnp.stack(
        [((x + nx - s) % nx) * nc + k for s in range(nx) for k in (c, (c + 1) % nc)]
    ).astype(jnp.int32)

    sums = pl.pallas_call(
        sum_factors,
        out_shape=jax.ShapeDtypeStruct((ny, held_rows, width), BF),
        in_specs=[in_smem, in_smem, in_smem, in_vmem],
        out_specs=in_vmem,
        scratch_shapes=[VMEM((targets * panels, rank, width), F32)],
        compiler_params=params(24),
        cost_estimate=pl.CostEstimate(flops=10**7, bytes_accessed=7 * 10**6, transcendentals=0),
        name="sum_factors",
    )(entry_panel[:, 0], entry_target[:, 0], entry_count[0], factors)

    packed, shared = pl.pallas_call(
        project,
        out_shape=(
            jax.ShapeDtypeStruct((ny, held_rows, width), BF),
            jax.ShapeDtypeStruct((rows + 2 * TAIL, width), BF),
        ),
        in_specs=[in_smem] + [in_vmem] * (nx + 2) + [in_any],
        out_specs=(in_any, in_vmem),
        scratch_shapes=[VMEM((ny, TAIL, width), BF), pltpu.SemaphoreType.DMA],
        input_output_aliases={nx + 3: 0},
        compiler_params=params(24),
        name="project",
    )(columns, *pieces, probes.reshape(targets * rank, width), coupling, sums)

    held = lax.all_to_all(packed, "y", 0, 0, tiled=True)
    shared, held = lax.optimization_barrier((shared, held))
    all_shared = lax.all_gather(shared, "y", axis=0, tiled=False)

    cut = width // nz
    sketch = pl.pallas_call(
        first_pass,
        out_shape=jax.ShapeDtypeStruct((nz, mine * rank, cut), F32),
        in_specs=[in_vmem],
        out_specs=in_vmem,
        compiler_params=params(24),
        name="first_pass",
    )(held)
    parts = lax.all_to_all(sketch, "z", 0, 0, tiled=True)
    copies = pl.pallas_call(
        add_up,
        out_shape=jax.ShapeDtypeStruct((nz, mine * rank, cut), F32),
        in_specs=[in_vmem],
        out_specs=in_vmem,
        name="add_up",
    )(parts)
    sketches = lax.all_to_all(copies, "z", 0, 0, tiled=True)

    keep = width // (ny * nz)
    rounded, *left = pl.pallas_call(
        orthonormal,
        out_shape=(jax.ShapeDtypeStruct((mine * rank, width), BF),)
        + (jax.ShapeDtypeStruct((keep, mine * rank), F32),) * ny,
        in_specs=[in_smem, in_vmem],
        out_specs=(in_vmem,) * (ny + 1),
        scratch_shapes=[VMEM((mine * rank, width), F32), VMEM((LANES, mine * rank), F32)],
        compiler_params=params(24),
        name="orthonormal",
    )(place, sketches)
    left_parts = [left[0]] + [
        lax.ppermute(left[s], "y", [(i, (i + s) % ny) for i in range(ny)]) for s in range(1, ny)
    ]
    rows_part = pl.pallas_call(
        second_pass,
        out_shape=jax.ShapeDtypeStruct((width, mine * rank), BF),
        in_specs=[in_vmem] * 3,
        out_specs=in_vmem,
        compiler_params=params(24),
        name="second_pass",
    )(held, rounded, all_shared)
    row_parts = lax.all_to_all(rows_part.reshape(ny * nz, keep, mine * rank), ("y", "z"), 0, 0, tiled=True)
    out = jax.ShapeDtypeStruct((targets, keep, rank), F32)
    left_out, right_out = pl.pallas_call(
        finish,
        out_shape=(out, out),
        in_specs=[in_smem] + [in_vmem] * (ny + 1),
        out_specs=(in_vmem, in_vmem),
        name="finish",
    )(place, row_parts, *left_parts)
    return left_out.transpose(0, 2, 1), right_out.transpose(0, 2, 1)


def solution(mesh):
    wide, narrow = mesh.devices.shape
    sizes = (4, wide // 4, narrow // 2, 2)
    axes = ("y", "z", "x", "core")
    finer = Mesh(mesh.devices.reshape(sizes), axes)
    split, owner = ("y", "z"), ("x", "core")
    placed = (
        P(split, owner, None, None),
        P(split, owner),
        P(split, owner),
        P(owner, split),
        P(split, None, owner),
        P(split, None, None),
        P(owner, None, None),
    )
    return jax.shard_map(
        functools.partial(shards, sizes),
        mesh=finer,
        in_specs=placed,
        out_specs=(P(owner, None, split), P(owner, None, split)),
        check_vma=False,
    )
```

```python
import functools
import math

import jax
import jax.numpy as jnp
from jax import lax
from jax.experimental import pallas as pl
from jax.experimental.pallas import tpu as pltpu
from jax.sharding import Mesh
from jax.sharding import PartitionSpec as P

BF = jnp.bfloat16
F32 = jnp.float32
HIGHEST = lax.Precision.HIGHEST
NT = (((1,), (1,)), ((), ()))
TN = (((0,), (0,)), ((), ()))
SMEM = pltpu.SMEM
VMEM = pltpu.VMEM
LANES = 128
TAIL = 16


def params(mib):
    return pltpu.CompilerParams(vmem_limit_bytes=mib * 1024 * 1024)


def split_bf(x, parts):
    out = []
    for _ in range(parts):
        part = x.astype(BF)
        out.append(part)
        x = x - part.astype(F32)
    return out


def pack_rows(block):
    return jnp.concatenate([block[q * TAIL : (q + 1) * TAIL] for q in range(block.shape[0] // TAIL)], axis=1)


def unpack_rows(ref, lead, row, first, count):
    return jnp.concatenate(
        [ref[lead, row : row + TAIL, q * LANES : (q + 1) * LANES] for q in range(first, first + count)], axis=0
    )


def sum_factors(panel, target, count, factors, out, loaded, acc, panel_at, target_at, count_at, sems, small):
    slots, rank, _ = loaded.shape
    pairs = acc.shape[0]
    panels = pairs // 8
    chunk = slots // sems.shape[0]
    indices = [
        pltpu.make_async_copy(source, to, small.at[i])
        for i, (source, to) in enumerate(((panel, panel_at), (target, target_at), (count, count_at)))
    ]
    for copy in indices:
        copy.start()
    loads = [
        pltpu.make_async_copy(factors.at[pl.ds(i * chunk, chunk)], loaded.at[pl.ds(i * chunk, chunk)], sems.at[i])
        for i in range(slots // chunk)
    ]
    for copy in loads:
        copy.start()

    def clear(i, _):
        acc[i] = jnp.zeros(acc.shape[1:], F32)
        return 0

    lax.fori_loop(0, pairs, clear, 0)
    for copy in indices:
        copy.wait()
    live = count_at[0]

    def add(e, _):
        pair = target_at[e] * panels + panel_at[e]
        acc[pair] += loaded[e].astype(F32)
        return 0

    for i, copy in enumerate(loads):
        copy.wait()
        lax.fori_loop(i * chunk, jnp.minimum(live, (i + 1) * chunk), add, 0)
    groups = out.shape[0]
    each = pairs // groups
    for i in range(pairs):
        row = (i % each) * rank
        out[i // each, row : row + rank, :] = acc[i].astype(BF)


def project(columns, *refs):
    pieces, refs = refs[:4], refs[4:]
    probes, coupling, shared, table = refs[0], refs[1], refs[2], refs[-1]
    sent = refs[3:-1]
    rows = pieces[0].shape[1]
    at = 0
    for piece in pieces:
        for half in range(piece.shape[0]):
            start = pl.multiple_of(columns[at] * LANES, LANES)
            shared[0:rows, pl.ds(start, LANES)] = piece[half]
            at += 1
    rank = coupling.shape[1]
    zero = jnp.zeros((rank, rank), F32)
    first, second = coupling[0], coupling[1]
    diagonal = jnp.concatenate(
        [jnp.concatenate([first, zero], axis=1), jnp.concatenate([zero, second], axis=1)], axis=0
    )
    projected = lax.dot_general(probes[...], shared[0:rows, :], NT, preferred_element_type=F32)
    table[...] = lax.dot_general(
        projected, diagonal, NT, precision=HIGHEST, preferred_element_type=F32
    ).astype(BF)
    each = sent[0].shape[0]
    for s in range(len(sent)):
        owner = lax.rem(columns[at] + s, len(sent))
        sent[s][...] = table[pl.ds(pl.multiple_of(owner * each, each), each), :]
    high, mid, low = split_bf(jnp.concatenate([first, second], axis=1), 3)
    shared[rows : rows + TAIL, :] = jnp.concatenate([pack_rows(high), pack_rows(mid)], axis=1)
    tail = pack_rows(low)
    shared[rows + TAIL : rows + 2 * TAIL, :] = jnp.concatenate([tail, jnp.zeros_like(tail)], axis=1)


def first_pass(place, held, *refs):
    coefficients, out = refs[:-1], refs[-1]
    groups, rows, width = held.shape
    targets = rows // LANES
    rank = out.shape[1] // targets
    cut = out.shape[2]
    for t in range(targets):
        total = jnp.zeros((rank, width), F32)
        for s in range(groups):
            source = lax.rem(place[0] + groups - s, groups)
            total = total + jnp.dot(
                coefficients[s][t * rank : (t + 1) * rank, :],
                held[source, t * LANES : (t + 1) * LANES, :],
                preferred_element_type=F32,
            )
        for z in range(out.shape[0]):
            out[z, t * rank : (t + 1) * rank, :] = total[:, z * cut : (z + 1) * cut]


def add_up(parts, out):
    total = parts[0]
    for z in range(1, parts.shape[0]):
        total = total + parts[z]
    for z in range(out.shape[0]):
        out[z] = total


def inverse_factors(grams):
    rank = grams[0].shape[0]
    row_at = lax.broadcasted_iota(jnp.int32, (rank, 2 * rank), 0)
    lane_at = lax.broadcasted_iota(jnp.int32, (rank, 2 * rank), 1)
    eye = (row_at + rank == lane_at).astype(F32)
    tables = [jnp.concatenate([g, jnp.zeros((rank, rank), F32)], axis=1) + eye for g in grams]
    scales = [jnp.ones((rank, 2 * rank), F32) for _ in grams]
    for k in range(rank):
        for i, table in enumerate(tables):
            top = (k // 8) * 8
            pivot_row = table[k : k + 1, :]
            pivot = pivot_row[:, k : k + 1]
            scaled = pivot_row * (1.0 / pivot)
            column = table[top:, k : k + 1]
            below = row_at[top:, :] > k
            lower = table[top:, :] - jnp.where(below, column * scaled, 0.0)
            tables[i] = lower if top == 0 else jnp.concatenate([table[:top], lower], axis=0)
            scales[i] = jnp.where(row_at == k, pivot, scales[i])
    return [(table * lax.rsqrt(scale))[:, rank:] for table, scale in zip(tables, scales, strict=True)]


def second_pass(place, sketches, held_far, *refs):
    groups = held_far.shape[0]
    shared_far, out, left, refs = refs[:groups], refs[groups], refs[groups + 1 : 2 * groups + 1], refs[2 * groups + 1 :]
    basis, rounded, turned, held, shared, sems = refs
    loads = [pltpu.make_async_copy(held_far, held, sems.at[groups])]
    loads += [pltpu.make_async_copy(shared_far[s], shared.at[s], sems.at[s]) for s in range(groups)]
    for copy in loads:
        copy.start()
    cuts, rows, _ = sketches.shape
    width = basis.shape[1]
    targets = held.shape[1] // LANES
    rank = rows // targets
    own = left[0].shape[0]
    whole = [
        jnp.concatenate([sketches[z, t * rank : (t + 1) * rank, :] for z in range(cuts)], axis=1)
        for t in range(targets)
    ]
    grams = [lax.dot_general(s, s, NT, precision=HIGHEST, preferred_element_type=F32) for s in whole]
    inverses = inverse_factors(grams)
    for t in range(targets):
        found = jnp.dot(inverses[t], whole[t], precision=HIGHEST, preferred_element_type=F32)
        basis[t * rank : (t + 1) * rank, :] = found
        rounded[t * rank : (t + 1) * rank, :] = found.astype(BF)
    for copy in loads:
        copy.wait()
    total = jnp.zeros((rows, width), F32)
    for s in range(groups):
        source = lax.rem(place[0] + groups - s, groups)
        summed = jnp.concatenate(
            [
                lax.dot_general(
                    held[source, t * LANES : (t + 1) * LANES, :],
                    rounded[t * rank : (t + 1) * rank, :],
                    NT,
                    preferred_element_type=F32,
                )
                for t in range(targets)
            ],
            axis=1,
        )
        coupling = (
            unpack_rows(shared, s, LANES, 0, 4).astype(F32) + unpack_rows(shared, s, LANES, 4, 4).astype(F32)
        ) + unpack_rows(shared, s, LANES + TAIL, 0, 4).astype(F32)
        middle = jnp.concatenate(
            [
                lax.dot_general(
                    coupling[:, d * rank : (d + 1) * rank],
                    summed[d * rank : (d + 1) * rank, :],
                    TN,
                    precision=HIGHEST,
                    preferred_element_type=F32,
                )
                for d in range(LANES // rank)
            ],
            axis=0,
        ).T
        for part in split_bf(middle, 2):
            total = total + jnp.dot(part, shared[s, 0:LANES, :], preferred_element_type=F32)
    for c in range(width // LANES):
        out[c * LANES : (c + 1) * LANES, :] = total[:, c * LANES : (c + 1) * LANES].T.astype(out.dtype)
    for s in range(groups):
        owner = lax.rem(place[0] + s, groups)
        start = owner * (width // groups) + place[1] * own
        aligned = (start // LANES) * LANES
        turned[...] = basis[:, pl.ds(pl.multiple_of(aligned, LANES), LANES)].T
        left[s][...] = turned[pl.ds(pl.multiple_of(start - aligned, 32), own), :]


def finish(place, parts, *refs):
    left_parts, (left, right) = refs[:-2], refs[-2:]
    owners = len(left_parts)
    groups = parts.shape[0] // owners
    targets = left.shape[0] // owners
    rank = left.shape[2]
    root = math.sqrt(1024)
    for y in range(owners):
        total = parts[y * groups].astype(F32)
        for z in range(1, groups):
            total = total + parts[y * groups + z].astype(F32)
        total = total / root
        for t in range(targets):
            right[y * targets + t] = total[:, t * rank : (t + 1) * rank]
    for s in range(owners):
        owner = lax.rem(place[0] + owners - s, owners)
        rows = left_parts[s][...] * root
        for t in range(targets):
            left[owner * targets + t] = rows[:, t * rank : (t + 1) * rank]


def shards(sizes, entry_factor, entry_panel, entry_target, entry_count, panel_shared, coupling, probes):
    ny, nz, nx, nc = sizes
    y, z = lax.axis_index("y"), lax.axis_index("z")
    x, c = lax.axis_index("x"), lax.axis_index("core")
    place = jnp.stack([y, z]).astype(jnp.int32)
    factors = entry_factor[:, 0]
    slots, rank, width = factors.shape
    panels = panel_shared.shape[0]
    targets = probes.shape[0]
    rows = panels * rank
    mine = targets // ny
    own_rows = mine * rank
    held_rows = mine * panels * rank
    in_vmem = pl.BlockSpec(memory_space=VMEM)
    in_smem = pl.BlockSpec(memory_space=SMEM)
    in_any = pl.BlockSpec(memory_space=pl.ANY)

    def turn(value, axis, size, by):
        return lax.ppermute(value, axis, [(i, (i + by) % size) for i in range(size)])

    sums = pl.pallas_call(
        sum_factors,
        out_shape=jax.ShapeDtypeStruct((ny, held_rows, width), BF),
        in_specs=[in_any] * 4,
        out_specs=in_vmem,
        scratch_shapes=[
            VMEM((slots, rank, width), BF),
            VMEM((targets * panels, rank, width), F32),
            SMEM((slots,), jnp.int32),
            SMEM((slots,), jnp.int32),
            SMEM((1,), jnp.int32),
            pltpu.SemaphoreType.DMA((6,)),
            pltpu.SemaphoreType.DMA((3,)),
        ],
        compiler_params=params(56),
        cost_estimate=pl.CostEstimate(flops=10**7, bytes_accessed=7 * 10**6, transcendentals=0),
        name="sum_factors",
    )(entry_panel[:, 0], entry_target[:, 0], entry_count[0], factors)
    held = lax.all_to_all(sums, "y", 0, 0, tiled=True)

    own, _ = lax.optimization_barrier((panel_shared.reshape(rows, LANES), sums))
    pair = jnp.stack([own, turn(own, "core", nc, 1)])
    pieces = [pair] + [turn(pair, "x", nx, s) for s in range(1, nx)]
    columns = jnp.stack(
        [((x + nx - s) % nx) * nc + k for s in range(nx) for k in (c, (c + 1) % nc)] + [y]
    ).astype(jnp.int32)
    shared, *sent = pl.pallas_call(
        project,
        out_shape=(jax.ShapeDtypeStruct((rows + 2 * TAIL, width), BF),)
        + (jax.ShapeDtypeStruct((own_rows, rows), BF),) * ny,
        in_specs=[in_smem] + [in_vmem] * (nx + 2),
        out_specs=(in_vmem,) * (ny + 1),
        scratch_shapes=[VMEM((targets * rank, rows), BF)],
        compiler_params=params(24),
        name="project",
    )(columns, *pieces, probes.reshape(targets * rank, width), coupling)
    coefficients = [sent[0]] + [turn(sent[s], "y", ny, s) for s in range(1, ny)]

    cut = width // nz
    sketch = pl.pallas_call(
        first_pass,
        out_shape=jax.ShapeDtypeStruct((nz, own_rows, cut), F32),
        in_specs=[in_smem] + [in_vmem] * (ny + 1),
        out_specs=in_vmem,
        compiler_params=params(24),
        name="first_pass",
    )(place, held, *coefficients)
    shared, sketch = lax.optimization_barrier((shared, sketch))
    all_shared = [shared] + [turn(shared, "y", ny, s) for s in range(1, ny)]
    parts = lax.all_to_all(sketch, "z", 0, 0, tiled=True)
    copies = pl.pallas_call(
        add_up,
        out_shape=jax.ShapeDtypeStruct((nz, own_rows, cut), F32),
        in_specs=[in_vmem],
        out_specs=in_vmem,
        name="add_up",
    )(parts)
    sketches = lax.all_to_all(copies, "z", 0, 0, tiled=True)

    keep = width // (ny * nz)
    rows_part, *left = pl.pallas_call(
        second_pass,
        out_shape=(jax.ShapeDtypeStruct((width, own_rows), BF),)
        + (jax.ShapeDtypeStruct((keep, own_rows), F32),) * ny,
        in_specs=[in_smem, in_vmem] + [in_any] * (ny + 1),
        out_specs=(in_vmem,) * (ny + 1),
        scratch_shapes=[
            VMEM((own_rows, width), F32),
            VMEM((own_rows, width), BF),
            VMEM((LANES, own_rows), F32),
            VMEM((ny, held_rows, width), BF),
            VMEM((ny, rows + 2 * TAIL, width), BF),
            pltpu.SemaphoreType.DMA((ny + 1,)),
        ],
        compiler_params=params(40),
        name="second_pass",
    )(place, sketches, held, *all_shared)
    left_parts = [left[0]] + [turn(left[s], "y", ny, s) for s in range(1, ny)]
    row_parts = lax.all_to_all(rows_part.reshape(ny * nz, keep, own_rows), ("y", "z"), 0, 0, tiled=True)
    out = jax.ShapeDtypeStruct((targets, keep, rank), F32)
    left_out, right_out = pl.pallas_call(
        finish,
        out_shape=(out, out),
        in_specs=[in_smem] + [in_vmem] * (ny + 1),
        out_specs=(in_vmem, in_vmem),
        name="finish",
    )(place, row_parts, *left_parts)
    return left_out.transpose(0, 2, 1), right_out.transpose(0, 2, 1)


def solution(mesh):
    wide, narrow = mesh.devices.shape
    sizes = (4, wide // 4, narrow // 2, 2)
    axes = ("y", "z", "x", "core")
    finer = Mesh(mesh.devices.reshape(sizes), axes)
    split, owner = ("y", "z"), ("x", "core")
    placed = (
        P(split, owner, None, None),
        P(split, owner),
        P(split, owner),
        P(owner, split),
        P(split, None, owner),
        P(split, None, None),
        P(owner, None, None),
    )
    return jax.shard_map(
        functools.partial(shards, sizes),
        mesh=finer,
        in_specs=placed,
        out_specs=(P(owner, None, split), P(owner, None, split)),
        check_vma=False,
    )
```

```python
import functools
import math

import jax
import jax.numpy as jnp
from jax import lax
from jax.experimental import pallas as pl
from jax.experimental.pallas import tpu as pltpu
from jax.sharding import Mesh
from jax.sharding import PartitionSpec as P

BF = jnp.bfloat16
F32 = jnp.float32
HIGHEST = lax.Precision.HIGHEST
NT = (((1,), (1,)), ((), ()))
TN = (((0,), (0,)), ((), ()))
SMEM = pltpu.SMEM
VMEM = pltpu.VMEM
LANES = 128
TAIL = 16
BLOCK = 4


def params(mib):
    return pltpu.CompilerParams(vmem_limit_bytes=mib * 1024 * 1024)


def split_bf(x, parts):
    out = []
    for _ in range(parts):
        part = x.astype(BF)
        out.append(part)
        x = x - part.astype(F32)
    return out


def pack_rows(block):
    return jnp.concatenate([block[q * TAIL : (q + 1) * TAIL] for q in range(block.shape[0] // TAIL)], axis=1)


def unpack_rows(ref, lead, row, first, count):
    return jnp.concatenate(
        [ref[lead, row : row + TAIL, q * LANES : (q + 1) * LANES] for q in range(first, first + count)], axis=0
    )


def sum_factors(panel, target, count, factors, out, loaded, acc, panel_at, target_at, count_at, sems, small):
    slots, rank, _ = loaded.shape
    pairs = acc.shape[0]
    panels = pairs // 8
    chunk = slots // sems.shape[0]
    indices = [
        pltpu.make_async_copy(source, to, small.at[i])
        for i, (source, to) in enumerate(((panel, panel_at), (target, target_at), (count, count_at)))
    ]
    for copy in indices:
        copy.start()
    loads = [
        pltpu.make_async_copy(factors.at[pl.ds(i * chunk, chunk)], loaded.at[pl.ds(i * chunk, chunk)], sems.at[i])
        for i in range(slots // chunk)
    ]
    for copy in loads:
        copy.start()

    def clear(i, _):
        acc[i] = jnp.zeros(acc.shape[1:], F32)
        return 0

    lax.fori_loop(0, pairs, clear, 0)
    for copy in indices:
        copy.wait()
    live = count_at[0]

    def add(e, _):
        pair = target_at[e] * panels + panel_at[e]
        acc[pair] += loaded[e].astype(F32)
        return 0

    for i, copy in enumerate(loads):
        copy.wait()
        lax.fori_loop(i * chunk, jnp.minimum(live, (i + 1) * chunk), add, 0)
    groups = out.shape[0]
    each = pairs // groups
    for i in range(pairs):
        row = (i % each) * rank
        out[i // each, row : row + rank, :] = acc[i].astype(BF)


def project(columns, *refs):
    pieces, refs = refs[:4], refs[4:]
    probes, coupling, shared, table = refs[0], refs[1], refs[2], refs[-1]
    sent = refs[3:-1]
    rows = pieces[0].shape[1]
    at = 0
    for piece in pieces:
        for half in range(piece.shape[0]):
            start = pl.multiple_of(columns[at] * LANES, LANES)
            shared[0:rows, pl.ds(start, LANES)] = piece[half]
            at += 1
    rank = coupling.shape[1]
    zero = jnp.zeros((rank, rank), F32)
    first, second = coupling[0], coupling[1]
    diagonal = jnp.concatenate(
        [jnp.concatenate([first, zero], axis=1), jnp.concatenate([zero, second], axis=1)], axis=0
    )
    projected = lax.dot_general(probes[...], shared[0:rows, :], NT, preferred_element_type=F32)
    table[...] = lax.dot_general(
        projected, diagonal, NT, precision=HIGHEST, preferred_element_type=F32
    ).astype(BF)
    each = sent[0].shape[0]
    for s in range(len(sent)):
        owner = lax.rem(columns[at] + s, len(sent))
        sent[s][...] = table[pl.ds(pl.multiple_of(owner * each, each), each), :]
    high, mid, low = split_bf(jnp.concatenate([first, second], axis=1), 3)
    shared[rows : rows + TAIL, :] = jnp.concatenate([pack_rows(high), pack_rows(mid)], axis=1)
    tail = pack_rows(low)
    shared[rows + TAIL : rows + 2 * TAIL, :] = jnp.concatenate([tail, jnp.zeros_like(tail)], axis=1)


def first_pass(place, held, *refs):
    coefficients, out = refs[:-1], refs[-1]
    groups, rows, width = held.shape
    targets = rows // LANES
    rank = out.shape[1] // targets
    cut = out.shape[2]
    for t in range(targets):
        total = jnp.zeros((rank, width), F32)
        for s in range(groups):
            source = lax.rem(place[0] + groups - s, groups)
            total = total + jnp.dot(
                coefficients[s][t * rank : (t + 1) * rank, :],
                held[source, t * LANES : (t + 1) * LANES, :],
                preferred_element_type=F32,
            )
        for z in range(out.shape[0]):
            out[z, t * rank : (t + 1) * rank, :] = total[:, z * cut : (z + 1) * cut]


def add_up(parts, out):
    total = parts[0].astype(F32)
    for z in range(1, parts.shape[0]):
        total = total + parts[z].astype(F32)
    for z in range(out.shape[0]):
        out[z] = total.astype(out.dtype)


def inverse_factors(grams):
    rank = grams[0].shape[0]
    row_at = lax.broadcasted_iota(jnp.int32, (rank, 2 * rank), 0)
    lane_at = lax.broadcasted_iota(jnp.int32, (rank, 2 * rank), 1)
    eye = (row_at + rank == lane_at).astype(F32)
    tables = [jnp.concatenate([g, jnp.zeros((rank, rank), F32)], axis=1) + eye for g in grams]
    for first in range(0, rank, BLOCK):
        top = (first // 8) * 8
        at = first - top
        for i, table in enumerate(tables):
            lower = table[top:, :]
            columns = [
                jnp.broadcast_to(lower[:, first + j : first + j + 1], lower.shape) for j in range(BLOCK)
            ]
            pivots = [lower[at + j : at + j + 1, :] for j in range(BLOCK)]
            for j in range(BLOCK):
                own = columns[j][at + j : at + j + 1, :]
                share = jnp.where(row_at[top:, :] > first + j, columns[j] * (1.0 / own), 0.0)
                for k in range(j + 1, BLOCK):
                    columns[k] = columns[k] - share * columns[j][at + k : at + k + 1, :]
                    pivots[k] = pivots[k] - share[at + k : at + k + 1, :] * pivots[j]
                lower = lower - share * pivots[j]
            tables[i] = lower if top == 0 else jnp.concatenate([table[:top], lower], axis=0)
    diagonal = row_at == lane_at
    return [
        (table * lax.rsqrt(jnp.sum(jnp.where(diagonal, table, 0.0), axis=1, keepdims=True)))[:, rank:]
        for table in tables
    ]


def second_pass(place, sketches, held_far, *refs):
    groups = held_far.shape[0]
    shared_far, out, left, refs = refs[:groups], refs[groups], refs[groups + 1 : 2 * groups + 1], refs[2 * groups + 1 :]
    basis, rounded, turned, held, shared, sems = refs
    loads = [pltpu.make_async_copy(held_far, held, sems.at[groups])]
    loads += [pltpu.make_async_copy(shared_far[s], shared.at[s], sems.at[s]) for s in range(groups)]
    for copy in loads:
        copy.start()
    cuts, rows, _ = sketches.shape
    width = basis.shape[1]
    targets = held.shape[1] // LANES
    rank = rows // targets
    own = left[0].shape[0]
    whole = [
        jnp.concatenate([sketches[z, t * rank : (t + 1) * rank, :] for z in range(cuts)], axis=1)
        for t in range(targets)
    ]
    grams = [lax.dot_general(s, s, NT, preferred_element_type=F32) for s in whole]
    inverses = inverse_factors(grams)
    for t in range(targets):
        found = jnp.dot(
            jnp.concatenate(split_bf(inverses[t], 3), axis=0), whole[t], preferred_element_type=F32
        )
        found = (found[0:rank] + found[rank : 2 * rank]) + found[2 * rank : 3 * rank]
        basis[t * rank : (t + 1) * rank, :] = found
        rounded[t * rank : (t + 1) * rank, :] = found.astype(BF)
    for copy in loads:
        copy.wait()
    total = jnp.zeros((rows, width), F32)
    for s in range(groups):
        source = lax.rem(place[0] + groups - s, groups)
        summed = jnp.concatenate(
            [
                lax.dot_general(
                    held[source, t * LANES : (t + 1) * LANES, :],
                    rounded[t * rank : (t + 1) * rank, :],
                    NT,
                    preferred_element_type=F32,
                )
                for t in range(targets)
            ],
            axis=1,
        )
        coupling = (
            unpack_rows(shared, s, LANES, 0, 4).astype(F32) + unpack_rows(shared, s, LANES, 4, 4).astype(F32)
        ) + unpack_rows(shared, s, LANES + TAIL, 0, 4).astype(F32)
        middle = jnp.concatenate(
            [
                lax.dot_general(
                    coupling[:, d * rank : (d + 1) * rank],
                    summed[d * rank : (d + 1) * rank, :],
                    TN,
                    precision=HIGHEST,
                    preferred_element_type=F32,
                )
                for d in range(LANES // rank)
            ],
            axis=0,
        ).T
        for part in split_bf(middle, 2):
            total = total + jnp.dot(part, shared[s, 0:LANES, :], preferred_element_type=F32)
    for c in range(width // LANES):
        out[c * LANES : (c + 1) * LANES, :] = total[:, c * LANES : (c + 1) * LANES].T.astype(out.dtype)
    for s in range(groups):
        owner = lax.rem(place[0] + s, groups)
        start = owner * (width // groups) + place[1] * own
        aligned = (start // LANES) * LANES
        turned[...] = basis[:, pl.ds(pl.multiple_of(aligned, LANES), LANES)].T
        left[s][...] = turned[pl.ds(pl.multiple_of(start - aligned, 32), own), :]


def finish(place, parts, *refs):
    left_parts, (left, right) = refs[:-2], refs[-2:]
    owners = len(left_parts)
    groups = parts.shape[0] // owners
    targets = left.shape[0] // owners
    rank = left.shape[2]
    root = math.sqrt(1024)
    for y in range(owners):
        total = parts[y * groups].astype(F32)
        for z in range(1, groups):
            total = total + parts[y * groups + z].astype(F32)
        total = total / root
        for t in range(targets):
            right[y * targets + t] = total[:, t * rank : (t + 1) * rank]
    for s in range(owners):
        owner = lax.rem(place[0] + owners - s, owners)
        rows = left_parts[s][...] * root
        for t in range(targets):
            left[owner * targets + t] = rows[:, t * rank : (t + 1) * rank]


def shards(sizes, entry_factor, entry_panel, entry_target, entry_count, panel_shared, coupling, probes):
    ny, nz, nx, nc = sizes
    y, z = lax.axis_index("y"), lax.axis_index("z")
    x, c = lax.axis_index("x"), lax.axis_index("core")
    place = jnp.stack([y, z]).astype(jnp.int32)
    factors = entry_factor[:, 0]
    slots, rank, width = factors.shape
    panels = panel_shared.shape[0]
    targets = probes.shape[0]
    rows = panels * rank
    mine = targets // ny
    own_rows = mine * rank
    held_rows = mine * panels * rank
    in_vmem = pl.BlockSpec(memory_space=VMEM)
    in_smem = pl.BlockSpec(memory_space=SMEM)
    in_any = pl.BlockSpec(memory_space=pl.ANY)

    def turn(value, axis, size, by):
        return lax.ppermute(value, axis, [(i, (i + by) % size) for i in range(size)])

    sums = pl.pallas_call(
        sum_factors,
        out_shape=jax.ShapeDtypeStruct((ny, held_rows, width), BF),
        in_specs=[in_any] * 4,
        out_specs=in_vmem,
        scratch_shapes=[
            VMEM((slots, rank, width), BF),
            VMEM((targets * panels, rank, width), F32),
            SMEM((slots,), jnp.int32),
            SMEM((slots,), jnp.int32),
            SMEM((1,), jnp.int32),
            pltpu.SemaphoreType.DMA((6,)),
            pltpu.SemaphoreType.DMA((3,)),
        ],
        compiler_params=params(56),
        cost_estimate=pl.CostEstimate(flops=10**7, bytes_accessed=7 * 10**6, transcendentals=0),
        name="sum_factors",
    )(entry_panel[:, 0], entry_target[:, 0], entry_count[0], factors)
    held = lax.all_to_all(sums, "y", 0, 0, tiled=True)

    own, _ = lax.optimization_barrier((panel_shared.reshape(rows, LANES), sums))
    pair = jnp.stack([own, turn(own, "core", nc, 1)])
    pieces = [pair] + [turn(pair, "x", nx, s) for s in range(1, nx)]
    columns = jnp.stack(
        [((x + nx - s) % nx) * nc + k for s in range(nx) for k in (c, (c + 1) % nc)] + [y]
    ).astype(jnp.int32)
    shared, *sent = pl.pallas_call(
        project,
        out_shape=(jax.ShapeDtypeStruct((rows + 2 * TAIL, width), BF),)
        + (jax.ShapeDtypeStruct((own_rows, rows), BF),) * ny,
        in_specs=[in_smem] + [in_vmem] * (nx + 2),
        out_specs=(in_vmem,) * (ny + 1),
        scratch_shapes=[VMEM((targets * rank, rows), BF)],
        compiler_params=params(60),
        name="project",
    )(columns, *pieces, probes.reshape(targets * rank, width), coupling)
    coefficients = [sent[0]] + [turn(sent[s], "y", ny, s) for s in range(1, ny)]

    cut = width // nz
    sketch = pl.pallas_call(
        first_pass,
        out_shape=jax.ShapeDtypeStruct((nz, own_rows, cut), F32),
        in_specs=[in_smem] + [in_vmem] * (ny + 1),
        out_specs=in_vmem,
        compiler_params=params(20),
        name="first_pass",
    )(place, held, *coefficients)
    shared, sketch = lax.optimization_barrier((shared, sketch))
    near = [turn(shared, "y", ny, s) for s in (1, ny - 1)]
    parts = lax.all_to_all(sketch, "z", 0, 0, tiled=True)
    parts, shared, *near = lax.optimization_barrier((parts, shared, *near))
    all_shared = [shared, near[0]] + [turn(shared, "y", ny, s) for s in range(2, ny - 1)] + [near[1]]
    copies = pl.pallas_call(
        add_up,
        out_shape=jax.ShapeDtypeStruct((nz, own_rows, cut), BF),
        in_specs=[in_vmem],
        out_specs=in_vmem,
        compiler_params=params(8),
        name="add_up",
    )(parts)
    sketches = lax.all_to_all(copies, "z", 0, 0, tiled=True)

    keep = width // (ny * nz)
    rows_part, *left = pl.pallas_call(
        second_pass,
        out_shape=(jax.ShapeDtypeStruct((width, own_rows), BF),)
        + (jax.ShapeDtypeStruct((keep, own_rows), F32),) * ny,
        in_specs=[in_smem, in_vmem] + [in_any] * (ny + 1),
        out_specs=(in_vmem,) * (ny + 1),
        scratch_shapes=[
            VMEM((own_rows, width), F32),
            VMEM((own_rows, width), BF),
            VMEM((LANES, own_rows), F32),
            VMEM((ny, held_rows, width), BF),
            VMEM((ny, rows + 2 * TAIL, width), BF),
            pltpu.SemaphoreType.DMA((ny + 1,)),
        ],
        compiler_params=params(52),
        name="second_pass",
    )(place, sketches, held, *all_shared)
    left_parts = [left[0]] + [turn(left[s], "y", ny, s) for s in range(1, ny)]
    row_parts = lax.all_to_all(rows_part.reshape(ny * nz, keep, own_rows), ("y", "z"), 0, 0, tiled=True)
    out = jax.ShapeDtypeStruct((targets, keep, rank), F32)
    left_out, right_out = pl.pallas_call(
        finish,
        out_shape=(out, out),
        in_specs=[in_smem] + [in_vmem] * (ny + 1),
        out_specs=(in_vmem, in_vmem),
        compiler_params=params(8),
        name="finish",
    )(place, row_parts, *left_parts)
    return left_out.transpose(0, 2, 1), right_out.transpose(0, 2, 1)


def solution(mesh):
    wide, narrow = mesh.devices.shape
    sizes = (4, wide // 4, narrow // 2, 2)
    axes = ("y", "z", "x", "core")
    finer = Mesh(mesh.devices.reshape(sizes), axes)
    split, owner = ("y", "z"), ("x", "core")
    placed = (
        P(split, owner, None, None),
        P(split, owner),
        P(split, owner),
        P(owner, split),
        P(split, None, owner),
        P(split, None, None),
        P(owner, None, None),
    )
    return jax.shard_map(
        functools.partial(shards, sizes),
        mesh=finer,
        in_specs=placed,
        out_specs=(P(owner, None, split), P(owner, None, split)),
        check_vma=False,
    )
```

```python
import functools
import math

import jax
import jax.numpy as jnp
from jax import lax
from jax.experimental import pallas as pl
from jax.experimental.pallas import tpu as pltpu
from jax.sharding import Mesh
from jax.sharding import PartitionSpec as P

BF = jnp.bfloat16
F32 = jnp.float32
HIGHEST = lax.Precision.HIGHEST
NT = (((1,), (1,)), ((), ()))
TN = (((0,), (0,)), ((), ()))
SMEM = pltpu.SMEM
VMEM = pltpu.VMEM
LANES = 128
TAIL = 16
BLOCK = 4


def params(mib):
    return pltpu.CompilerParams(vmem_limit_bytes=mib * 1024 * 1024)


def split_bf(x, parts):
    out = []
    for _ in range(parts):
        part = x.astype(BF)
        out.append(part)
        x = x - part.astype(F32)
    return out


def pack_rows(block):
    return jnp.concatenate([block[q * TAIL : (q + 1) * TAIL] for q in range(block.shape[0] // TAIL)], axis=1)


def unpack_rows(ref, lead, row, first, count):
    return jnp.concatenate(
        [ref[lead, row : row + TAIL, q * LANES : (q + 1) * LANES] for q in range(first, first + count)], axis=0
    )


def sum_factors(panel, target, count, factors, out, loaded, acc, panel_at, target_at, count_at, sems, small):
    slots, rank, _ = loaded.shape
    pairs = acc.shape[0]
    panels = pairs // 8
    chunk = slots // sems.shape[0]
    indices = [
        pltpu.make_async_copy(source, to, small.at[i])
        for i, (source, to) in enumerate(((panel, panel_at), (target, target_at), (count, count_at)))
    ]
    for copy in indices:
        copy.start()
    loads = [
        pltpu.make_async_copy(factors.at[pl.ds(i * chunk, chunk)], loaded.at[pl.ds(i * chunk, chunk)], sems.at[i])
        for i in range(slots // chunk)
    ]
    for copy in loads:
        copy.start()

    def clear(i, _):
        acc[i] = jnp.zeros(acc.shape[1:], F32)
        return 0

    lax.fori_loop(0, pairs, clear, 0)
    for copy in indices:
        copy.wait()
    live = count_at[0]

    def add(e, _):
        pair = target_at[e] * panels + panel_at[e]
        acc[pair] += loaded[e].astype(F32)
        return 0

    for i, copy in enumerate(loads):
        copy.wait()
        lax.fori_loop(i * chunk, jnp.minimum(live, (i + 1) * chunk), add, 0)
    groups = out.shape[0]
    each = pairs // groups
    for i in range(pairs):
        row = (i % each) * rank
        out[i // each, row : row + rank, :] = acc[i].astype(BF)


def project(columns, *refs):
    pieces, refs = refs[:4], refs[4:]
    probes, coupling, shared, table = refs[0], refs[1], refs[2], refs[-1]
    sent = refs[3:-1]
    rows = pieces[0].shape[1]
    at = 0
    for piece in pieces:
        for half in range(piece.shape[0]):
            start = pl.multiple_of(columns[at] * LANES, LANES)
            shared[0:rows, pl.ds(start, LANES)] = piece[half]
            at += 1
    rank = coupling.shape[1]
    zero = jnp.zeros((rank, rank), F32)
    first, second = coupling[0], coupling[1]
    diagonal = jnp.concatenate(
        [jnp.concatenate([first, zero], axis=1), jnp.concatenate([zero, second], axis=1)], axis=0
    )
    projected = lax.dot_general(probes[...], shared[0:rows, :], NT, preferred_element_type=F32)
    table[...] = lax.dot_general(
        projected, diagonal, NT, precision=HIGHEST, preferred_element_type=F32
    ).astype(BF)
    each = sent[0].shape[0]
    for s in range(len(sent)):
        owner = lax.rem(columns[at] + s, len(sent))
        sent[s][...] = table[pl.ds(pl.multiple_of(owner * each, each), each), :]
    high, mid, low = split_bf(jnp.concatenate([first, second], axis=1), 3)
    shared[rows : rows + TAIL, :] = jnp.concatenate([pack_rows(high), pack_rows(mid)], axis=1)
    tail = pack_rows(low)
    shared[rows + TAIL : rows + 2 * TAIL, :] = jnp.concatenate([tail, jnp.zeros_like(tail)], axis=1)


def first_pass(place, held, *refs):
    coefficients, out = refs[:-1], refs[-1]
    groups, rows, width = held.shape
    targets = rows // LANES
    rank = out.shape[1] // targets
    cut = out.shape[2]
    for t in range(targets):
        total = jnp.zeros((rank, width), F32)
        for s in range(groups):
            source = lax.rem(place[0] + groups - s, groups)
            total = total + jnp.dot(
                coefficients[s][t * rank : (t + 1) * rank, :],
                held[source, t * LANES : (t + 1) * LANES, :],
                preferred_element_type=F32,
            )
        for z in range(out.shape[0]):
            out[z, t * rank : (t + 1) * rank, :] = total[:, z * cut : (z + 1) * cut].astype(BF)


def add_up(parts, out):
    total = parts[0].astype(F32)
    for z in range(1, parts.shape[0]):
        total = total + parts[z].astype(F32)
    for z in range(out.shape[0]):
        out[z] = total.astype(out.dtype)


def inverse_factors(grams):
    rank = grams[0].shape[0]
    row_at = lax.broadcasted_iota(jnp.int32, (rank, 2 * rank), 0)
    lane_at = lax.broadcasted_iota(jnp.int32, (rank, 2 * rank), 1)
    eye = (row_at + rank == lane_at).astype(F32)
    tables = [jnp.concatenate([g, jnp.zeros((rank, rank), F32)], axis=1) + eye for g in grams]
    for first in range(0, rank, BLOCK):
        top = (first // 8) * 8
        at = first - top
        for i, table in enumerate(tables):
            lower = table[top:, :]
            columns = [
                jnp.broadcast_to(lower[:, first + j : first + j + 1], lower.shape) for j in range(BLOCK)
            ]
            pivots = [lower[at + j : at + j + 1, :] for j in range(BLOCK)]
            for j in range(BLOCK):
                own = columns[j][at + j : at + j + 1, :]
                share = jnp.where(row_at[top:, :] > first + j, columns[j] * (1.0 / own), 0.0)
                for k in range(j + 1, BLOCK):
                    columns[k] = columns[k] - share * columns[j][at + k : at + k + 1, :]
                    pivots[k] = pivots[k] - share[at + k : at + k + 1, :] * pivots[j]
                lower = lower - share * pivots[j]
            tables[i] = lower if top == 0 else jnp.concatenate([table[:top], lower], axis=0)
    diagonal = row_at == lane_at
    return [
        (table * lax.rsqrt(jnp.sum(jnp.where(diagonal, table, 0.0), axis=1, keepdims=True)))[:, rank:]
        for table in tables
    ]


def second_pass(place, sketches, held_far, *refs):
    groups = held_far.shape[0]
    shared_far, out, left, refs = refs[:5], refs[5], refs[6 : 6 + groups], refs[6 + groups :]
    basis, rounded, turned, held, shared, sems = refs
    half = shared.shape[1] // 2
    targets_of = (
        shared.at[0],
        shared.at[1],
        shared.at[2, 0:half, :],
        shared.at[2, half : 2 * half, :],
        shared.at[3],
    )
    loads = [pltpu.make_async_copy(held_far, held, sems.at[5])]
    loads += [
        pltpu.make_async_copy(source, to, sems.at[i])
        for i, (source, to) in enumerate(zip(shared_far, targets_of, strict=True))
    ]
    for copy in loads:
        copy.start()
    cuts, rows, _ = sketches.shape
    width = basis.shape[1]
    targets = held.shape[1] // LANES
    rank = rows // targets
    own = left[0].shape[0]
    whole = [
        jnp.concatenate([sketches[z, t * rank : (t + 1) * rank, :] for z in range(cuts)], axis=1)
        for t in range(targets)
    ]
    grams = [lax.dot_general(s, s, NT, preferred_element_type=F32) for s in whole]
    inverses = inverse_factors(grams)
    for t in range(targets):
        found = jnp.dot(
            jnp.concatenate(split_bf(inverses[t], 3), axis=0), whole[t], preferred_element_type=F32
        )
        found = (found[0:rank] + found[rank : 2 * rank]) + found[2 * rank : 3 * rank]
        basis[t * rank : (t + 1) * rank, :] = found
        rounded[t * rank : (t + 1) * rank, :] = found.astype(BF)
    for copy in loads:
        copy.wait()
    total = jnp.zeros((rows, width), F32)
    for s in range(groups):
        source = lax.rem(place[0] + groups - s, groups)
        summed = jnp.concatenate(
            [
                lax.dot_general(
                    held[source, t * LANES : (t + 1) * LANES, :],
                    rounded[t * rank : (t + 1) * rank, :],
                    NT,
                    preferred_element_type=F32,
                )
                for t in range(targets)
            ],
            axis=1,
        )
        coupling = (
            unpack_rows(shared, s, LANES, 0, 4).astype(F32) + unpack_rows(shared, s, LANES, 4, 4).astype(F32)
        ) + unpack_rows(shared, s, LANES + TAIL, 0, 4).astype(F32)
        middle = jnp.concatenate(
            [
                lax.dot_general(
                    coupling[:, d * rank : (d + 1) * rank],
                    summed[d * rank : (d + 1) * rank, :],
                    TN,
                    precision=HIGHEST,
                    preferred_element_type=F32,
                )
                for d in range(LANES // rank)
            ],
            axis=0,
        ).T
        for part in split_bf(middle, 2):
            total = total + jnp.dot(part, shared[s, 0:LANES, :], preferred_element_type=F32)
    for c in range(width // LANES):
        out[c * LANES : (c + 1) * LANES, :] = total[:, c * LANES : (c + 1) * LANES].T.astype(out.dtype)
    for s in range(groups):
        owner = lax.rem(place[0] + s, groups)
        start = owner * (width // groups) + place[1] * own
        aligned = (start // LANES) * LANES
        turned[...] = basis[:, pl.ds(pl.multiple_of(aligned, LANES), LANES)].T
        left[s][...] = turned[pl.ds(pl.multiple_of(start - aligned, 32), own), :]


def finish(place, parts, *refs):
    left_parts, (left, right) = refs[:-2], refs[-2:]
    owners = len(left_parts)
    groups = parts.shape[0] // owners
    targets = left.shape[0] // owners
    rank = left.shape[2]
    root = math.sqrt(1024)
    for y in range(owners):
        total = parts[y * groups].astype(F32)
        for z in range(1, groups):
            total = total + parts[y * groups + z].astype(F32)
        total = total / root
        for t in range(targets):
            right[y * targets + t] = total[:, t * rank : (t + 1) * rank]
    for s in range(owners):
        owner = lax.rem(place[0] + owners - s, owners)
        rows = left_parts[s][...] * root
        for t in range(targets):
            left[owner * targets + t] = rows[:, t * rank : (t + 1) * rank]


def shards(sizes, entry_factor, entry_panel, entry_target, entry_count, panel_shared, coupling, probes):
    ny, nz, nx, nc = sizes
    y, z = lax.axis_index("y"), lax.axis_index("z")
    x, c = lax.axis_index("x"), lax.axis_index("core")
    place = jnp.stack([y, z]).astype(jnp.int32)
    factors = entry_factor[:, 0]
    slots, rank, width = factors.shape
    panels = panel_shared.shape[0]
    targets = probes.shape[0]
    rows = panels * rank
    mine = targets // ny
    own_rows = mine * rank
    held_rows = mine * panels * rank
    in_vmem = pl.BlockSpec(memory_space=VMEM)
    in_smem = pl.BlockSpec(memory_space=SMEM)
    in_any = pl.BlockSpec(memory_space=pl.ANY)

    def turn(value, axis, size, by):
        return lax.ppermute(value, axis, [(i, (i + by) % size) for i in range(size)])

    sums = pl.pallas_call(
        sum_factors,
        out_shape=jax.ShapeDtypeStruct((ny, held_rows, width), BF),
        in_specs=[in_any] * 4,
        out_specs=in_vmem,
        scratch_shapes=[
            VMEM((slots, rank, width), BF),
            VMEM((targets * panels, rank, width), F32),
            SMEM((slots,), jnp.int32),
            SMEM((slots,), jnp.int32),
            SMEM((1,), jnp.int32),
            pltpu.SemaphoreType.DMA((6,)),
            pltpu.SemaphoreType.DMA((3,)),
        ],
        compiler_params=params(56),
        cost_estimate=pl.CostEstimate(flops=10**7, bytes_accessed=7 * 10**6, transcendentals=0),
        name="sum_factors",
    )(entry_panel[:, 0], entry_target[:, 0], entry_count[0], factors)
    held = lax.all_to_all(sums, "y", 0, 0, tiled=True)

    own, _ = lax.optimization_barrier((panel_shared.reshape(rows, LANES), sums))
    pair = jnp.stack([own, turn(own, "core", nc, 1)])
    pieces = [pair] + [turn(pair, "x", nx, s) for s in range(1, nx)]
    columns = jnp.stack(
        [((x + nx - s) % nx) * nc + k for s in range(nx) for k in (c, (c + 1) % nc)] + [y]
    ).astype(jnp.int32)
    shared, *sent = pl.pallas_call(
        project,
        out_shape=(jax.ShapeDtypeStruct((rows + 2 * TAIL, width), BF),)
        + (jax.ShapeDtypeStruct((own_rows, rows), BF),) * ny,
        in_specs=[in_smem] + [in_vmem] * (nx + 2),
        out_specs=(in_vmem,) * (ny + 1),
        scratch_shapes=[VMEM((targets * rank, rows), BF)],
        compiler_params=params(60),
        name="project",
    )(columns, *pieces, probes.reshape(targets * rank, width), coupling)
    coefficients = [sent[0]] + [turn(sent[s], "y", ny, s) for s in range(1, ny)]

    cut = width // nz
    sketch = pl.pallas_call(
        first_pass,
        out_shape=jax.ShapeDtypeStruct((nz, own_rows, cut), BF),
        in_specs=[in_smem] + [in_vmem] * (ny + 1),
        out_specs=in_vmem,
        compiler_params=params(20),
        name="first_pass",
    )(place, held, *coefficients)
    shared, sketch = lax.optimization_barrier((shared, sketch))
    near = [turn(shared, "y", ny, s) for s in (1, ny - 1)]
    parts = lax.all_to_all(sketch, "z", 0, 0, tiled=True)
    parts, shared, *near = lax.optimization_barrier((parts, shared, *near))
    middle_row = shared.shape[0] // 2
    far = [turn(near[0][:middle_row], "y", ny, 1), turn(near[1][middle_row:], "y", ny, ny - 1)]
    all_shared = [shared, near[0], *far, near[1]]
    copies = pl.pallas_call(
        add_up,
        out_shape=jax.ShapeDtypeStruct((nz, own_rows, cut), BF),
        in_specs=[in_vmem],
        out_specs=in_vmem,
        compiler_params=params(8),
        name="add_up",
    )(parts)
    sketches = lax.all_to_all(copies, "z", 0, 0, tiled=True)

    keep = width // (ny * nz)
    rows_part, *left = pl.pallas_call(
        second_pass,
        out_shape=(jax.ShapeDtypeStruct((width, own_rows), BF),)
        + (jax.ShapeDtypeStruct((keep, own_rows), F32),) * ny,
        in_specs=[in_smem, in_vmem] + [in_any] * 6,
        out_specs=(in_vmem,) * (ny + 1),
        scratch_shapes=[
            VMEM((own_rows, width), F32),
            VMEM((own_rows, width), BF),
            VMEM((LANES, own_rows), F32),
            VMEM((ny, held_rows, width), BF),
            VMEM((ny, rows + 2 * TAIL, width), BF),
            pltpu.SemaphoreType.DMA((6,)),
        ],
        compiler_params=params(52),
        name="second_pass",
    )(place, sketches, held, *all_shared)
    left_parts = [left[0]] + [turn(left[s], "y", ny, s) for s in range(1, ny)]
    row_parts = lax.all_to_all(rows_part.reshape(ny * nz, keep, own_rows), ("y", "z"), 0, 0, tiled=True)
    out = jax.ShapeDtypeStruct((targets, keep, rank), F32)
    left_out, right_out = pl.pallas_call(
        finish,
        out_shape=(out, out),
        in_specs=[in_smem] + [in_vmem] * (ny + 1),
        out_specs=(in_vmem, in_vmem),
        compiler_params=params(8),
        name="finish",
    )(place, row_parts, *left_parts)
    return left_out.transpose(0, 2, 1), right_out.transpose(0, 2, 1)


def solution(mesh):
    wide, narrow = mesh.devices.shape
    sizes = (4, wide // 4, narrow // 2, 2)
    axes = ("y", "z", "x", "core")
    finer = Mesh(mesh.devices.reshape(sizes), axes)
    split, owner = ("y", "z"), ("x", "core")
    placed = (
        P(split, owner, None, None),
        P(split, owner),
        P(split, owner),
        P(owner, split),
        P(split, None, owner),
        P(split, None, None),
        P(owner, None, None),
    )
    return jax.shard_map(
        functools.partial(shards, sizes),
        mesh=finer,
        in_specs=placed,
        out_specs=(P(owner, None, split), P(owner, None, split)),
        check_vma=False,
    )
```

```python
import functools
import math

import jax
import jax.numpy as jnp
from jax import lax
from jax.experimental import pallas as pl
from jax.experimental.pallas import tpu as pltpu
from jax.sharding import Mesh
from jax.sharding import PartitionSpec as P

BF = jnp.bfloat16
F32 = jnp.float32
HIGHEST = lax.Precision.HIGHEST
NT = (((1,), (1,)), ((), ()))
TN = (((0,), (0,)), ((), ()))
SMEM = pltpu.SMEM
VMEM = pltpu.VMEM
LANES = 128
TAIL = 16
BLOCK = 8


def params(mib):
    return pltpu.CompilerParams(vmem_limit_bytes=mib * 1024 * 1024)


def split_bf(x, parts):
    out = []
    for _ in range(parts):
        part = x.astype(BF)
        out.append(part)
        x = x - part.astype(F32)
    return out


def pack_rows(block):
    return jnp.concatenate([block[q * TAIL : (q + 1) * TAIL] for q in range(block.shape[0] // TAIL)], axis=1)


def unpack_rows(ref, lead, row, first, count):
    return jnp.concatenate(
        [ref[lead, row : row + TAIL, q * LANES : (q + 1) * LANES] for q in range(first, first + count)], axis=0
    )


def sum_factors(panel, target, count, factors, out, loaded, acc, kept, panel_at, target_at, count_at, sems, small):
    slots, rank, _ = loaded.shape
    pairs = acc.shape[0]
    panels = pairs // 8
    chunk = slots // 6
    indices = [
        pltpu.make_async_copy(source, to, small.at[i])
        for i, (source, to) in enumerate(((panel, panel_at), (target, target_at), (count, count_at)))
    ]
    for copy in indices:
        copy.start()
    loads = [
        pltpu.make_async_copy(factors.at[pl.ds(i * chunk, chunk)], loaded.at[pl.ds(i * chunk, chunk)], sems.at[i])
        for i in range(slots // chunk)
    ]
    for copy in loads:
        copy.start()

    def clear(i, _):
        acc[i] = jnp.zeros(acc.shape[1:], F32)
        return 0

    lax.fori_loop(0, pairs, clear, 0)
    for copy in indices:
        copy.wait()
    live = count_at[0]

    def add(e, _):
        pair = target_at[e] * panels + panel_at[e]
        acc[pair] += loaded[e].astype(F32)
        return 0

    for i, copy in enumerate(loads):
        copy.wait()
        lax.fori_loop(i * chunk, jnp.minimum(live, (i + 1) * chunk), add, 0)
    groups = out.shape[0]
    each = pairs // groups
    stores = [pltpu.make_async_copy(kept.at[g], out.at[g], sems.at[6 + g]) for g in range(groups)]
    for g, copy in enumerate(stores):
        for i in range(each):
            kept[g, i * rank : (i + 1) * rank, :] = acc[g * each + i].astype(BF)
        copy.start()
    for copy in stores:
        copy.wait()


def project(columns, *refs):
    pieces, refs = refs[:4], refs[4:]
    probes, coupling, shared, table = refs[0], refs[1], refs[2], refs[-1]
    sent = refs[3:-1]
    rows = pieces[0].shape[1]
    at = 0
    for piece in pieces:
        for half in range(piece.shape[0]):
            start = pl.multiple_of(columns[at] * LANES, LANES)
            shared[0:rows, pl.ds(start, LANES)] = piece[half]
            at += 1
    rank = coupling.shape[1]
    zero = jnp.zeros((rank, rank), F32)
    first, second = coupling[0], coupling[1]
    diagonal = jnp.concatenate(
        [jnp.concatenate([first, zero], axis=1), jnp.concatenate([zero, second], axis=1)], axis=0
    )
    projected = lax.dot_general(probes[...], shared[0:rows, :], NT, preferred_element_type=F32)
    table[...] = lax.dot_general(
        projected, diagonal, NT, precision=HIGHEST, preferred_element_type=F32
    ).astype(BF)
    each = sent[0].shape[0]
    for s in range(len(sent)):
        owner = lax.rem(columns[at] + s, len(sent))
        sent[s][...] = table[pl.ds(pl.multiple_of(owner * each, each), each), :]
    high, mid, low = split_bf(jnp.concatenate([first, second], axis=1), 3)
    shared[rows : rows + TAIL, :] = jnp.concatenate([pack_rows(high), pack_rows(mid)], axis=1)
    tail = pack_rows(low)
    shared[rows + TAIL : rows + 2 * TAIL, :] = jnp.concatenate([tail, jnp.zeros_like(tail)], axis=1)


def first_pass(place, held, *refs):
    coefficients, out = refs[:-1], refs[-1]
    groups, rows, width = held.shape
    targets = rows // LANES
    rank = out.shape[1] // targets
    cut = out.shape[2]
    for t in range(targets):
        total = jnp.zeros((rank, width), F32)
        for s in range(groups):
            source = lax.rem(place[0] + groups - s, groups)
            total = total + jnp.dot(
                coefficients[s][t * rank : (t + 1) * rank, :],
                held[source, t * LANES : (t + 1) * LANES, :],
                preferred_element_type=F32,
            )
        for z in range(out.shape[0]):
            out[z, t * rank : (t + 1) * rank, :] = total[:, z * cut : (z + 1) * cut].astype(BF)


def add_up(parts, out):
    total = parts[0].astype(F32)
    for z in range(1, parts.shape[0]):
        total = total + parts[z].astype(F32)
    for z in range(out.shape[0]):
        out[z] = total.astype(out.dtype)


def inverse_factors(grams):
    rank = grams[0].shape[0]
    row_at = lax.broadcasted_iota(jnp.int32, (rank, 2 * rank), 0)
    lane_at = lax.broadcasted_iota(jnp.int32, (rank, 2 * rank), 1)
    eye = (row_at + rank == lane_at).astype(F32)
    tables = [jnp.concatenate([g, jnp.zeros((rank, rank), F32)], axis=1) + eye for g in grams]
    for first in range(0, rank, BLOCK):
        top = (first // 8) * 8
        at = first - top
        for i, table in enumerate(tables):
            lower = table[top:, :]
            columns = [
                jnp.broadcast_to(lower[:, first + j : first + j + 1], lower.shape) for j in range(BLOCK)
            ]
            pivots = [lower[at + j : at + j + 1, :] for j in range(BLOCK)]
            for j in range(BLOCK):
                own = columns[j][at + j : at + j + 1, :]
                share = jnp.where(row_at[top:, :] > first + j, columns[j] * (1.0 / own), 0.0)
                for k in range(j + 1, BLOCK):
                    columns[k] = columns[k] - share * columns[j][at + k : at + k + 1, :]
                    pivots[k] = pivots[k] - share[at + k : at + k + 1, :] * pivots[j]
                lower = lower - share * pivots[j]
            tables[i] = lower if top == 0 else jnp.concatenate([table[:top], lower], axis=0)
    diagonal = row_at == lane_at
    return [
        (table * lax.rsqrt(jnp.sum(jnp.where(diagonal, table, 0.0), axis=1, keepdims=True)))[:, rank:]
        for table in tables
    ]


def second_pass(place, sketches, held_far, *refs):
    groups = held_far.shape[0]
    shared_far, (out, held, shared, sems) = refs[:5], refs[5:]
    half = shared.shape[1] // 2
    sources = [lax.rem(place[0] + groups - s, groups) for s in range(groups)]
    loads = [pltpu.make_async_copy(held_far.at[source], held.at[s], sems.at[s]) for s, source in enumerate(sources)]
    ends = (
        shared.at[0],
        shared.at[1],
        shared.at[2, 0:half, :],
        shared.at[2, half : 2 * half, :],
        shared.at[3],
    )
    panels = [
        pltpu.make_async_copy(source, to, sems.at[groups + i])
        for i, (source, to) in enumerate(zip(shared_far, ends, strict=True))
    ]
    arrivals = ((0,), (1,), (2, 3), (4,))
    for s in range(groups):
        loads[s].start()
        for i in arrivals[s]:
            panels[i].start()
    cuts, rows, _ = sketches.shape
    width = held.shape[2]
    targets = held.shape[1] // LANES
    rank = rows // targets
    whole = [
        jnp.concatenate([sketches[z, t * rank : (t + 1) * rank, :] for z in range(cuts)], axis=1)
        for t in range(targets)
    ]
    total = jnp.zeros((rows, width), F32)
    for s in range(groups):
        loads[s].wait()
        for i in arrivals[s]:
            panels[i].wait()
        summed = jnp.concatenate(
            [
                lax.dot_general(
                    held[s, t * LANES : (t + 1) * LANES, :], whole[t], NT, preferred_element_type=F32
                )
                for t in range(targets)
            ],
            axis=1,
        )
        coupling = (
            unpack_rows(shared, s, LANES, 0, 4).astype(F32) + unpack_rows(shared, s, LANES, 4, 4).astype(F32)
        ) + unpack_rows(shared, s, LANES + TAIL, 0, 4).astype(F32)
        middle = jnp.concatenate(
            [
                lax.dot_general(
                    coupling[:, d * rank : (d + 1) * rank],
                    summed[d * rank : (d + 1) * rank, :],
                    TN,
                    precision=HIGHEST,
                    preferred_element_type=F32,
                )
                for d in range(LANES // rank)
            ],
            axis=0,
        ).T
        for part in split_bf(middle, 2):
            total = total + jnp.dot(part, shared[s, 0:LANES, :], preferred_element_type=F32)
    for c in range(width // LANES):
        out[c * LANES : (c + 1) * LANES, :] = total[:, c * LANES : (c + 1) * LANES].T.astype(out.dtype)


def factor(place, sketches, *refs):
    sent, (turned,) = refs[:-1], refs[-1:]
    cuts, rows, cut = sketches.shape
    targets = 2
    rank = rows // targets
    whole = [
        jnp.concatenate([sketches[z, t * rank : (t + 1) * rank, :] for z in range(cuts)], axis=1)
        for t in range(targets)
    ]
    grams = [lax.dot_general(s, s, NT, preferred_element_type=F32) for s in whole]
    inverses = jnp.concatenate(inverse_factors(grams), axis=1)
    owners = len(sent)
    own = sent[0].shape[0] - rank
    for s in range(owners):
        owner = lax.rem(place[0] + s, owners)
        start = owner * (cuts * cut // owners) + place[1] * own
        piece = start // cut
        turned[...] = sketches[piece].astype(F32).T
        sent[s][0:rank, :] = inverses
        sent[s][rank : rank + own, :] = turned[pl.ds(pl.multiple_of(start - piece * cut, 32), own), :]


def finish(place, parts, *refs):
    received, (left, right) = refs[:-2], refs[-2:]
    owners = len(received)
    groups = parts.shape[0] // owners
    targets = left.shape[0] // owners
    own, rank = left.shape[1], left.shape[2]
    root = math.sqrt(1024)
    for s in range(owners):
        owner = lax.rem(place[0] + owners - s, owners)
        total = parts[owner * groups].astype(F32)
        for z in range(1, groups):
            total = total + parts[owner * groups + z].astype(F32)
        both = jnp.concatenate([received[s][rank : rank + own, :] * root, total / root], axis=0)
        for t in range(targets):
            found = lax.dot_general(
                both[:, t * rank : (t + 1) * rank],
                received[s][0:rank, t * rank : (t + 1) * rank],
                NT,
                precision=HIGHEST,
                preferred_element_type=F32,
            )
            left[owner * targets + t] = found[0:own]
            right[owner * targets + t] = found[own : 2 * own]


def shards(sizes, entry_factor, entry_panel, entry_target, entry_count, panel_shared, coupling, probes):
    ny, nz, nx, nc = sizes
    y, z = lax.axis_index("y"), lax.axis_index("z")
    x, c = lax.axis_index("x"), lax.axis_index("core")
    place = jnp.stack([y, z]).astype(jnp.int32)
    factors = entry_factor[:, 0]
    slots, rank, width = factors.shape
    panels = panel_shared.shape[0]
    targets = probes.shape[0]
    rows = panels * rank
    mine = targets // ny
    own_rows = mine * rank
    held_rows = mine * panels * rank
    in_vmem = pl.BlockSpec(memory_space=VMEM)
    in_smem = pl.BlockSpec(memory_space=SMEM)
    in_any = pl.BlockSpec(memory_space=pl.ANY)

    def turn(value, axis, size, by):
        return lax.ppermute(value, axis, [(i, (i + by) % size) for i in range(size)])

    sums = pl.pallas_call(
        sum_factors,
        out_shape=jax.ShapeDtypeStruct((ny, held_rows, width), BF),
        in_specs=[in_any] * 4,
        out_specs=in_any,
        scratch_shapes=[
            VMEM((slots, rank, width), BF),
            VMEM((targets * panels, rank, width), F32),
            VMEM((ny, held_rows, width), BF),
            SMEM((slots,), jnp.int32),
            SMEM((slots,), jnp.int32),
            SMEM((1,), jnp.int32),
            pltpu.SemaphoreType.DMA((6 + ny,)),
            pltpu.SemaphoreType.DMA((3,)),
        ],
        compiler_params=params(56),
        cost_estimate=pl.CostEstimate(flops=10**7, bytes_accessed=7 * 10**6, transcendentals=0),
        name="sum_factors",
    )(entry_panel[:, 0], entry_target[:, 0], entry_count[0], factors)
    held = lax.all_to_all(sums, "y", 0, 0, tiled=True)

    own, _ = lax.optimization_barrier((panel_shared.reshape(rows, LANES), sums))
    pair = jnp.stack([own, turn(own, "core", nc, 1)])
    pieces = [pair] + [turn(pair, "x", nx, s) for s in range(1, nx)]
    columns = jnp.stack(
        [((x + nx - s) % nx) * nc + k for s in range(nx) for k in (c, (c + 1) % nc)] + [y]
    ).astype(jnp.int32)
    shared, *sent = pl.pallas_call(
        project,
        out_shape=(jax.ShapeDtypeStruct((rows + 2 * TAIL, width), BF),)
        + (jax.ShapeDtypeStruct((own_rows, rows), BF),) * ny,
        in_specs=[in_smem] + [in_vmem] * (nx + 2),
        out_specs=(in_vmem,) * (ny + 1),
        scratch_shapes=[VMEM((targets * rank, rows), BF)],
        compiler_params=params(60),
        name="project",
    )(columns, *pieces, probes.reshape(targets * rank, width), coupling)
    coefficients = [sent[0]] + [turn(sent[s], "y", ny, s) for s in range(1, ny)]

    cut = width // nz
    sketch = pl.pallas_call(
        first_pass,
        out_shape=jax.ShapeDtypeStruct((nz, own_rows, cut), BF),
        in_specs=[in_smem] + [in_vmem] * (ny + 1),
        out_specs=in_vmem,
        compiler_params=params(20),
        name="first_pass",
    )(place, held, *coefficients)
    shared, sketch = lax.optimization_barrier((shared, sketch))
    near = [turn(shared, "y", ny, s) for s in (1, ny - 1)]
    parts = lax.all_to_all(sketch, "z", 0, 0, tiled=True)
    parts, shared, *near = lax.optimization_barrier((parts, shared, *near))
    middle_row = shared.shape[0] // 2
    far = [turn(near[0][:middle_row], "y", ny, 1), turn(near[1][middle_row:], "y", ny, ny - 1)]
    all_shared = [shared, near[0], *far, near[1]]
    copies = pl.pallas_call(
        add_up,
        out_shape=jax.ShapeDtypeStruct((nz, own_rows, cut), BF),
        in_specs=[in_vmem],
        out_specs=in_vmem,
        compiler_params=params(8),
        name="add_up",
    )(parts)
    sketches = lax.all_to_all(copies, "z", 0, 0, tiled=True)

    keep = width // (ny * nz)
    rows_part = pl.pallas_call(
        second_pass,
        out_shape=jax.ShapeDtypeStruct((width, own_rows), BF),
        in_specs=[in_smem, in_vmem] + [in_any] * 6,
        out_specs=in_vmem,
        scratch_shapes=[
            VMEM((ny, held_rows, width), BF),
            VMEM((ny, rows + 2 * TAIL, width), BF),
            pltpu.SemaphoreType.DMA((ny + 5,)),
        ],
        compiler_params=params(52),
        name="second_pass",
    )(place, sketches, held, *all_shared)
    row_parts = lax.all_to_all(rows_part.reshape(ny * nz, keep, own_rows), ("y", "z"), 0, 0, tiled=True)
    sketches, _ = lax.optimization_barrier((sketches, rows_part))
    sent = pl.pallas_call(
        factor,
        out_shape=(jax.ShapeDtypeStruct((rank + keep, own_rows), F32),) * ny,
        in_specs=[in_smem, in_vmem],
        out_specs=(in_vmem,) * ny,
        scratch_shapes=[VMEM((cut, own_rows), F32)],
        compiler_params=params(8),
        cost_estimate=pl.CostEstimate(flops=10**7, bytes_accessed=5 * 10**5, transcendentals=0),
        name="factor",
    )(place, sketches)
    received = [sent[0]] + [turn(sent[s], "y", ny, s) for s in range(1, ny)]
    out = jax.ShapeDtypeStruct((targets, keep, rank), F32)
    left_out, right_out = pl.pallas_call(
        finish,
        out_shape=(out, out),
        in_specs=[in_smem] + [in_vmem] * (ny + 1),
        out_specs=(in_vmem, in_vmem),
        compiler_params=params(8),
        name="finish",
    )(place, row_parts, *received)
    return left_out.transpose(0, 2, 1), right_out.transpose(0, 2, 1)


def solution(mesh):
    wide, narrow = mesh.devices.shape
    sizes = (4, wide // 4, narrow // 2, 2)
    axes = ("y", "z", "x", "core")
    finer = Mesh(mesh.devices.reshape(sizes), axes)
    split, owner = ("y", "z"), ("x", "core")
    placed = (
        P(split, owner, None, None),
        P(split, owner),
        P(split, owner),
        P(owner, split),
        P(split, None, owner),
        P(split, None, None),
        P(owner, None, None),
    )
    return jax.shard_map(
        functools.partial(shards, sizes),
        mesh=finer,
        in_specs=placed,
        out_specs=(P(owner, None, split), P(owner, None, split)),
        check_vma=False,
    )
```

```python
import functools
import math

import jax
import jax.numpy as jnp
from jax import lax
from jax.experimental import pallas as pl
from jax.experimental.pallas import tpu as pltpu
from jax.sharding import Mesh
from jax.sharding import PartitionSpec as P

BF = jnp.bfloat16
F32 = jnp.float32
HIGHEST = lax.Precision.HIGHEST
NT = (((1,), (1,)), ((), ()))
TN = (((0,), (0,)), ((), ()))
SMEM = pltpu.SMEM
VMEM = pltpu.VMEM
LANES = 128
BLOCK = 8
TAIL = 16
RELAY = 80


def params(mib):
    return pltpu.CompilerParams(vmem_limit_bytes=mib * 1024 * 1024)


def split_bf(x, parts):
    out = []
    for _ in range(parts):
        part = x.astype(BF)
        out.append(part)
        x = x - part.astype(F32)
    return out


def pack_rows(block):
    return jnp.concatenate([block[q * TAIL : (q + 1) * TAIL] for q in range(block.shape[0] // TAIL)], axis=1)


def unpack_rows(block):
    return jnp.concatenate([block[:, q * LANES : (q + 1) * LANES] for q in range(block.shape[1] // LANES)], axis=0)


def sum_factors(panel, target, count, factors, out, loaded, acc, kept, panel_at, target_at, count_at, sems, small):
    slots, rank, _ = loaded.shape
    pairs = acc.shape[0]
    panels = pairs // 8
    chunk = slots // 6
    indices = [
        pltpu.make_async_copy(source, to, small.at[i])
        for i, (source, to) in enumerate(((panel, panel_at), (target, target_at), (count, count_at)))
    ]
    for copy in indices:
        copy.start()
    loads = [
        pltpu.make_async_copy(factors.at[pl.ds(i * chunk, chunk)], loaded.at[pl.ds(i * chunk, chunk)], sems.at[i])
        for i in range(slots // chunk)
    ]
    for copy in loads:
        copy.start()

    def clear(i, _):
        acc[i] = jnp.zeros(acc.shape[1:], F32)
        return 0

    lax.fori_loop(0, pairs, clear, 0)
    for copy in indices:
        copy.wait()
    live = count_at[0]

    def add(e, _):
        pair = target_at[e] * panels + panel_at[e]
        acc[pair] += loaded[e].astype(F32)
        return 0

    for i, copy in enumerate(loads):
        copy.wait()
        lax.fori_loop(i * chunk, jnp.minimum(live, (i + 1) * chunk), add, 0)
    groups = out.shape[0]
    each = pairs // groups
    stores = [pltpu.make_async_copy(kept.at[g], out.at[g], sems.at[6 + g]) for g in range(groups)]
    for g, copy in enumerate(stores):
        for i in range(each):
            kept[g, i * rank : (i + 1) * rank, :] = acc[g * each + i].astype(BF)
        copy.start()
    for copy in stores:
        copy.wait()


def project(columns, *refs):
    pieces, refs = refs[:4], refs[4:]
    probes, coupling, mine, other = refs[:4]
    sent, (shared, table) = refs[4:-2], refs[-2:]
    rows = pieces[0].shape[1]
    at = 0
    for piece in pieces:
        for half in range(piece.shape[0]):
            start = pl.multiple_of(columns[at] * LANES, LANES)
            shared[0:rows, pl.ds(start, LANES)] = piece[half]
            at += 1
    rank = coupling.shape[1]
    zero = jnp.zeros((rank, rank), F32)
    first, second = coupling[0], coupling[1]
    diagonal = jnp.concatenate(
        [jnp.concatenate([first, zero], axis=1), jnp.concatenate([zero, second], axis=1)], axis=0
    )
    projected = lax.dot_general(probes[...], shared[0:rows, :], NT, preferred_element_type=F32)
    table[...] = lax.dot_general(projected, diagonal, NT, precision=HIGHEST, preferred_element_type=F32)
    each = sent[0].shape[0]
    for s in range(len(sent)):
        owner = lax.rem(columns[at] + s, len(sent))
        sent[s][...] = table[pl.ds(pl.multiple_of(owner * each, each), each), :].astype(sent[s].dtype)
    high, low = split_bf(jnp.concatenate([first, second], axis=1), 2)
    shared[rows : rows + TAIL, :] = jnp.concatenate([pack_rows(high), pack_rows(low)], axis=1)
    half = mine.shape[1]
    core = columns[at + 1]
    mine[...] = shared[:, pl.ds(pl.multiple_of(core * half, half), half)]
    other[...] = shared[:, pl.ds(pl.multiple_of((1 - core) * half, half), half)]


def first_pass(place, held, *refs):
    coefficients, out = refs[:-1], refs[-1]
    groups, rows, width = held.shape
    targets = rows // LANES
    rank = out.shape[1] // targets
    cut = out.shape[2]
    totals = [jnp.zeros((rank, width), F32) for _ in range(targets)]
    for s in range(groups):
        source = lax.rem(place[0] + groups - s, groups)
        for t in range(targets):
            totals[t] = totals[t] + jnp.dot(
                coefficients[s][t * rank : (t + 1) * rank, :],
                held[source, t * LANES : (t + 1) * LANES, :],
                preferred_element_type=F32,
            )
    for t in range(targets):
        for z in range(out.shape[0]):
            out[z, t * rank : (t + 1) * rank, :] = totals[t][:, z * cut : (z + 1) * cut].astype(BF)


def add_up(parts, out):
    total = parts[0].astype(F32)
    for z in range(1, parts.shape[0]):
        total = total + parts[z].astype(F32)
    for z in range(out.shape[0]):
        out[z] = total.astype(out.dtype)


def inverse_factors(grams):
    rank = grams[0].shape[0]
    row_at = lax.broadcasted_iota(jnp.int32, (rank, 2 * rank), 0)
    lane_at = lax.broadcasted_iota(jnp.int32, (rank, 2 * rank), 1)
    eye = (row_at + rank == lane_at).astype(F32)
    tables = [jnp.concatenate([g, jnp.zeros((rank, rank), F32)], axis=1) + eye for g in grams]
    for first in range(0, rank, BLOCK):
        top = (first // 8) * 8
        at = first - top
        for i, table in enumerate(tables):
            lower = table[top:, :]
            columns = [
                jnp.broadcast_to(lower[:, first + j : first + j + 1], lower.shape) for j in range(BLOCK)
            ]
            pivots = [lower[at + j : at + j + 1, :] for j in range(BLOCK)]
            for j in range(BLOCK):
                own = columns[j][at + j : at + j + 1, :]
                share = jnp.where(row_at[top:, :] > first + j, columns[j] * (1.0 / own), 0.0)
                for k in range(j + 1, BLOCK):
                    columns[k] = columns[k] - share * columns[j][at + k : at + k + 1, :]
                    pivots[k] = pivots[k] - share[at + k : at + k + 1, :] * pivots[j]
                lower = lower - share * pivots[j]
            tables[i] = lower if top == 0 else jnp.concatenate([table[:top], lower], axis=0)
    diagonal = row_at == lane_at
    return [
        (table * lax.rsqrt(jnp.sum(jnp.where(diagonal, table, 0.0), axis=1, keepdims=True)))[:, rank:]
        for table in tables
    ]


def second_pass(place, sketches, held, *refs):
    groups = held.shape[0]
    out, sent, turned = refs[10], refs[11:-1], refs[-1]
    cuts, rows, cut = sketches.shape
    width = held.shape[2]
    targets = held.shape[1] // LANES
    rank = rows // targets
    whole = [
        jnp.concatenate([sketches[z, t * rank : (t + 1) * rank, :] for z in range(cuts)], axis=1)
        for t in range(targets)
    ]
    grams = [lax.dot_general(s, s, NT, preferred_element_type=F32) for s in whole]
    inverses = jnp.concatenate(inverse_factors(grams), axis=1)
    halves = [
        [
            refs[at][...],
            refs[at + 1][...],
            jnp.concatenate([refs[at + 2][...], refs[at + 3][...]], axis=0),
            refs[at + 4][...],
        ]
        for at in (0, 5)
    ]
    half = width // 2
    totals = [jnp.zeros((rows, half), F32) for _ in halves]
    for s in range(groups):
        source = lax.rem(place[0] + groups - s, groups)
        summed = jnp.concatenate(
            [
                lax.dot_general(
                    held[source, t * LANES : (t + 1) * LANES, :], whole[t], NT, preferred_element_type=F32
                )
                for t in range(targets)
            ],
            axis=1,
        )
        coupling = unpack_rows(halves[0][s][LANES:]).astype(F32) + unpack_rows(halves[1][s][LANES:]).astype(F32)
        middle = jnp.concatenate(
            [
                lax.dot_general(
                    coupling[:, d * rank : (d + 1) * rank],
                    summed[d * rank : (d + 1) * rank, :],
                    TN,
                    precision=HIGHEST,
                    preferred_element_type=F32,
                )
                for d in range(LANES // rank)
            ],
            axis=0,
        ).T
        for part in split_bf(middle, 2):
            for h, panels in enumerate(halves):
                totals[h] = totals[h] + jnp.dot(part, panels[s][0:LANES], preferred_element_type=F32)
    for h, total in enumerate(totals):
        side = place[2] if h == 0 else 1 - place[2]
        for c in range(half // LANES):
            start = pl.multiple_of(side * half + c * LANES, LANES)
            out[pl.ds(start, LANES), :] = total[:, c * LANES : (c + 1) * LANES].T.astype(out.dtype)
    own = sent[0].shape[0] - rank
    for s in range(groups):
        owner = lax.rem(place[0] + s, groups)
        start = owner * (width // groups) + place[1] * own
        piece = start // cut
        turned[...] = sketches[piece].astype(F32).T
        sent[s][0:rank, :] = inverses
        sent[s][rank : rank + own, :] = turned[pl.ds(pl.multiple_of(start - piece * cut, 32), own), :]


def finish(place, parts, *refs):
    received, (left, right) = refs[:-2], refs[-2:]
    owners = len(received)
    groups = parts.shape[0] // owners
    targets = left.shape[0] // owners
    own, rank = left.shape[1], left.shape[2]
    root = math.sqrt(1024)
    for s in range(owners):
        owner = lax.rem(place[0] + owners - s, owners)
        total = parts[owner * groups].astype(F32)
        for z in range(1, groups):
            total = total + parts[owner * groups + z].astype(F32)
        both = jnp.concatenate([received[s][rank : rank + own, :] * root, total / root], axis=0)
        for t in range(targets):
            found = lax.dot_general(
                both[:, t * rank : (t + 1) * rank],
                received[s][0:rank, t * rank : (t + 1) * rank],
                NT,
                precision=HIGHEST,
                preferred_element_type=F32,
            )
            left[owner * targets + t] = found[0:own]
            right[owner * targets + t] = found[own : 2 * own]


def shards(sizes, entry_factor, entry_panel, entry_target, entry_count, panel_shared, coupling, probes):
    ny, nz, nx, nc = sizes
    y, z = lax.axis_index("y"), lax.axis_index("z")
    x, c = lax.axis_index("x"), lax.axis_index("core")
    place = jnp.stack([y, z, c]).astype(jnp.int32)
    factors = entry_factor[:, 0]
    slots, rank, width = factors.shape
    panels = panel_shared.shape[0]
    targets = probes.shape[0]
    rows = panels * rank
    mine = targets // ny
    own_rows = mine * rank
    held_rows = mine * panels * rank
    in_vmem = pl.BlockSpec(memory_space=VMEM)
    in_smem = pl.BlockSpec(memory_space=SMEM)
    in_any = pl.BlockSpec(memory_space=pl.ANY)

    def turn(value, axis, size, by):
        return lax.ppermute(value, axis, [(i, (i + by) % size) for i in range(size)])

    sums = pl.pallas_call(
        sum_factors,
        out_shape=jax.ShapeDtypeStruct((ny, held_rows, width), BF),
        in_specs=[in_any] * 4,
        out_specs=in_any,
        scratch_shapes=[
            VMEM((slots, rank, width), BF),
            VMEM((targets * panels, rank, width), F32),
            VMEM((ny, held_rows, width), BF),
            SMEM((slots,), jnp.int32),
            SMEM((slots,), jnp.int32),
            SMEM((1,), jnp.int32),
            pltpu.SemaphoreType.DMA((6 + ny,)),
            pltpu.SemaphoreType.DMA((3,)),
        ],
        compiler_params=params(56),
        cost_estimate=pl.CostEstimate(flops=10**7, bytes_accessed=7 * 10**6, transcendentals=0),
        name="sum_factors",
    )(entry_panel[:, 0], entry_target[:, 0], entry_count[0], factors)
    held = lax.all_to_all(sums, "y", 0, 0, tiled=True)

    own, _ = lax.optimization_barrier((panel_shared.reshape(rows, LANES), sums))
    pair = jnp.stack([own, turn(own, "core", nc, 1)])
    pieces = [pair] + [turn(pair, "x", nx, s) for s in range(1, nx)]
    columns = jnp.stack(
        [((x + nx - s) % nx) * nc + k for s in range(nx) for k in (c, (c + 1) % nc)] + [y, c]
    ).astype(jnp.int32)
    mine_half, other_half, *sent = pl.pallas_call(
        project,
        out_shape=(jax.ShapeDtypeStruct((rows + TAIL, width // 2), BF),) * 2
        + (jax.ShapeDtypeStruct((own_rows, rows), F32),)
        + (jax.ShapeDtypeStruct((own_rows, rows), BF),) * (ny - 1),
        in_specs=[in_smem] + [in_vmem] * (nx + 2),
        out_specs=(in_vmem,) * (ny + 2),
        scratch_shapes=[VMEM((rows + TAIL, width), BF), VMEM((targets * rank, rows), F32)],
        compiler_params=params(60),
        name="project",
    )(columns, *pieces, probes.reshape(targets * rank, width), coupling)
    coefficients = [sent[0].astype(BF)] + [turn(sent[s], "y", ny, s) for s in range(1, ny)]

    cut = width // nz
    sketch = pl.pallas_call(
        first_pass,
        out_shape=jax.ShapeDtypeStruct((nz, own_rows, cut), BF),
        in_specs=[in_smem] + [in_vmem] * (ny + 1),
        out_specs=in_vmem,
        compiler_params=params(20),
        name="first_pass",
    )(place, held, *coefficients)
    mine_half, sketch = lax.optimization_barrier((mine_half, sketch))
    near = [turn(mine_half, "y", ny, s) for s in (1, ny - 1)]
    parts = lax.all_to_all(sketch, "z", 0, 0, tiled=True)
    parts, *near = lax.optimization_barrier((parts, *near))
    far = [turn(near[0][:RELAY], "y", ny, 1), turn(near[1][RELAY:], "y", ny, ny - 1)]
    halves = [near[0], *far, near[1]]
    all_shared = [mine_half, *halves, other_half] + [turn(h, "core", nc, 1) for h in halves]
    copies = pl.pallas_call(
        add_up,
        out_shape=jax.ShapeDtypeStruct((nz, own_rows, cut), BF),
        in_specs=[in_vmem],
        out_specs=in_vmem,
        compiler_params=params(8),
        name="add_up",
    )(parts)
    sketches = lax.all_to_all(copies, "z", 0, 0, tiled=True)

    keep = width // (ny * nz)
    rows_part, *sent = pl.pallas_call(
        second_pass,
        out_shape=(jax.ShapeDtypeStruct((width, own_rows), BF),)
        + (jax.ShapeDtypeStruct((rank + keep, own_rows), F32),) * ny,
        in_specs=[in_smem] + [in_vmem] * 12,
        out_specs=(in_vmem,) * (ny + 1),
        scratch_shapes=[VMEM((cut, own_rows), F32)],
        compiler_params=params(52),
        name="second_pass",
    )(place, sketches, held, *all_shared)
    row_parts = lax.all_to_all(rows_part.reshape(ny * nz, keep, own_rows), ("y", "z"), 0, 0, tiled=True)
    received = [sent[0]] + [turn(sent[s], "y", ny, s) for s in range(1, ny)]
    out = jax.ShapeDtypeStruct((targets, keep, rank), F32)
    left_out, right_out = pl.pallas_call(
        finish,
        out_shape=(out, out),
        in_specs=[in_smem] + [in_vmem] * (ny + 1),
        out_specs=(in_vmem, in_vmem),
        compiler_params=params(8),
        name="finish",
    )(place, row_parts, *received)
    return left_out.transpose(0, 2, 1), right_out.transpose(0, 2, 1)


def solution(mesh):
    wide, narrow = mesh.devices.shape
    sizes = (4, wide // 4, narrow // 2, 2)
    axes = ("y", "z", "x", "core")
    finer = Mesh(mesh.devices.reshape(sizes), axes)
    split, owner = ("y", "z"), ("x", "core")
    placed = (
        P(split, owner, None, None),
        P(split, owner),
        P(split, owner),
        P(owner, split),
        P(split, None, owner),
        P(split, None, None),
        P(owner, None, None),
    )
    return jax.shard_map(
        functools.partial(shards, sizes),
        mesh=finer,
        in_specs=placed,
        out_specs=(P(owner, None, split), P(owner, None, split)),
        check_vma=False,
    )
```

```python
import functools
import math

import jax
import jax.numpy as jnp
from jax import lax
from jax.experimental import pallas as pl
from jax.experimental.pallas import tpu as pltpu
from jax.sharding import Mesh
from jax.sharding import PartitionSpec as P

BF = jnp.bfloat16
F32 = jnp.float32
HIGHEST = lax.Precision.HIGHEST
NT = (((1,), (1,)), ((), ()))
TN = (((0,), (0,)), ((), ()))
SMEM = pltpu.SMEM
VMEM = pltpu.VMEM
LANES = 128
BLOCK = 8
TAIL = 16
RELAY = 80


def params(mib):
    return pltpu.CompilerParams(vmem_limit_bytes=mib * 1024 * 1024)


def split_bf(x, parts):
    out = []
    for _ in range(parts):
        part = x.astype(BF)
        out.append(part)
        x = x - part.astype(F32)
    return out


def pack_rows(block):
    return jnp.concatenate([block[q * TAIL : (q + 1) * TAIL] for q in range(block.shape[0] // TAIL)], axis=1)


def unpack_rows(block):
    return jnp.concatenate([block[:, q * LANES : (q + 1) * LANES] for q in range(block.shape[1] // LANES)], axis=0)


def sum_factors(panel, target, count, factors, *refs):
    out, (loaded, acc, kept, panel_at, target_at, count_at, sems, small) = refs[:-8], refs[-8:]
    slots, rank, _ = loaded.shape
    pairs = acc.shape[0]
    panels = pairs // 8
    chunk = slots // 6
    indices = [
        pltpu.make_async_copy(source, to, small.at[i])
        for i, (source, to) in enumerate(((panel, panel_at), (target, target_at), (count, count_at)))
    ]
    for copy in indices:
        copy.start()
    loads = [
        pltpu.make_async_copy(factors.at[pl.ds(i * chunk, chunk)], loaded.at[pl.ds(i * chunk, chunk)], sems.at[i])
        for i in range(slots // chunk)
    ]
    for copy in loads:
        copy.start()

    def clear(i, _):
        acc[i] = jnp.zeros(acc.shape[1:], F32)
        return 0

    lax.fori_loop(0, pairs, clear, 0)
    for copy in indices:
        copy.wait()
    live = count_at[0]

    def add(e, _):
        pair = target_at[e] * panels + panel_at[e]
        acc[pair] += loaded[e].astype(F32)
        return 0

    for i, copy in enumerate(loads):
        copy.wait()
        lax.fori_loop(i * chunk, jnp.minimum(live, (i + 1) * chunk), add, 0)
    groups = len(out)
    each = pairs // groups
    here = lax.axis_index("y")
    stores = [pltpu.make_async_copy(kept.at[s], out[s], sems.at[6 + s]) for s in range(groups)]
    for s in [*range(1, groups), 0]:
        owner = lax.rem(here + s, groups)
        for i in range(each):
            kept[s, i * rank : (i + 1) * rank, :] = acc[owner * each + i].astype(BF)
        stores[s].start()
    for copy in stores:
        copy.wait()


def project(columns, *refs):
    pieces, refs = refs[:4], refs[4:]
    probes, coupling, mine, other = refs[:4]
    sent, (shared, table) = refs[4:-2], refs[-2:]
    rows = pieces[0].shape[1]
    at = 0
    for piece in pieces:
        for half in range(piece.shape[0]):
            start = pl.multiple_of(columns[at] * LANES, LANES)
            shared[0:rows, pl.ds(start, LANES)] = piece[half]
            at += 1
    rank = coupling.shape[1]
    zero = jnp.zeros((rank, rank), F32)
    first, second = coupling[0], coupling[1]
    diagonal = jnp.concatenate(
        [jnp.concatenate([first, zero], axis=1), jnp.concatenate([zero, second], axis=1)], axis=0
    )
    projected = lax.dot_general(probes[...], shared[0:rows, :], NT, preferred_element_type=F32)
    table[...] = lax.dot_general(projected, diagonal, NT, precision=HIGHEST, preferred_element_type=F32)
    each = sent[0].shape[0]
    for s in range(len(sent)):
        owner = lax.rem(columns[at] + s, len(sent))
        sent[s][...] = table[pl.ds(pl.multiple_of(owner * each, each), each), :].astype(sent[s].dtype)
    high, low = split_bf(jnp.concatenate([first, second], axis=1), 2)
    shared[rows : rows + TAIL, :] = jnp.concatenate([pack_rows(high), pack_rows(low)], axis=1)
    half = mine.shape[1]
    core = columns[at + 1]
    mine[...] = shared[:, pl.ds(pl.multiple_of(core * half, half), half)]
    other[...] = shared[:, pl.ds(pl.multiple_of((1 - core) * half, half), half)]


def first_pass(*refs):
    groups = len(refs) // 2
    held, coefficients, out = refs[:groups], refs[groups:-1], refs[-1]
    rows, width = held[0].shape
    targets = rows // LANES
    rank = out.shape[1] // targets
    cut = out.shape[2]
    totals = [jnp.zeros((rank, width), F32) for _ in range(targets)]
    for s in range(groups):
        for t in range(targets):
            totals[t] = totals[t] + jnp.dot(
                coefficients[s][t * rank : (t + 1) * rank, :],
                held[s][t * LANES : (t + 1) * LANES, :],
                preferred_element_type=F32,
            )
    for t in range(targets):
        for z in range(out.shape[0]):
            out[z, t * rank : (t + 1) * rank, :] = totals[t][:, z * cut : (z + 1) * cut].astype(BF)


def add_up(parts, out):
    total = parts[0].astype(F32)
    for z in range(1, parts.shape[0]):
        total = total + parts[z].astype(F32)
    for z in range(out.shape[0]):
        out[z] = total.astype(out.dtype)


def inverse_factors(grams):
    rank = grams[0].shape[0]
    row_at = lax.broadcasted_iota(jnp.int32, (rank, 2 * rank), 0)
    lane_at = lax.broadcasted_iota(jnp.int32, (rank, 2 * rank), 1)
    eye = (row_at + rank == lane_at).astype(F32)
    tables = [jnp.concatenate([g, jnp.zeros((rank, rank), F32)], axis=1) + eye for g in grams]
    for first in range(0, rank, BLOCK):
        top = (first // 8) * 8
        at = first - top
        for i, table in enumerate(tables):
            lower = table[top:, :]
            columns = [
                jnp.broadcast_to(lower[:, first + j : first + j + 1], lower.shape) for j in range(BLOCK)
            ]
            pivots = [lower[at + j : at + j + 1, :] for j in range(BLOCK)]
            for j in range(BLOCK):
                own = columns[j][at + j : at + j + 1, :]
                share = jnp.where(row_at[top:, :] > first + j, columns[j] * (1.0 / own), 0.0)
                for k in range(j + 1, BLOCK):
                    columns[k] = columns[k] - share * columns[j][at + k : at + k + 1, :]
                    pivots[k] = pivots[k] - share[at + k : at + k + 1, :] * pivots[j]
                lower = lower - share * pivots[j]
            tables[i] = lower if top == 0 else jnp.concatenate([table[:top], lower], axis=0)
    diagonal = row_at == lane_at
    return [
        (table * lax.rsqrt(jnp.sum(jnp.where(diagonal, table, 0.0), axis=1, keepdims=True)))[:, rank:]
        for table in tables
    ]


def second_pass(place, sketches, *refs):
    held, refs = refs[:4], refs[4:]
    groups = len(held)
    out, sent, turned = refs[10], refs[11:-1], refs[-1]
    cuts, rows, cut = sketches.shape
    width = held[0].shape[1]
    targets = held[0].shape[0] // LANES
    rank = rows // targets
    whole = [
        jnp.concatenate([sketches[z, t * rank : (t + 1) * rank, :] for z in range(cuts)], axis=1)
        for t in range(targets)
    ]
    grams = [lax.dot_general(s, s, NT, preferred_element_type=F32) for s in whole]
    inverses = jnp.concatenate(inverse_factors(grams), axis=1)
    halves = [
        [
            refs[at][...],
            refs[at + 1][...],
            jnp.concatenate([refs[at + 2][...], refs[at + 3][...]], axis=0),
            refs[at + 4][...],
        ]
        for at in (0, 5)
    ]
    half = width // 2
    totals = [jnp.zeros((rows, half), F32) for _ in halves]
    for s in range(groups):
        summed = jnp.concatenate(
            [
                lax.dot_general(
                    held[s][t * LANES : (t + 1) * LANES, :], whole[t], NT, preferred_element_type=F32
                )
                for t in range(targets)
            ],
            axis=1,
        )
        coupling = unpack_rows(halves[0][s][LANES:]).astype(F32) + unpack_rows(halves[1][s][LANES:]).astype(F32)
        middle = jnp.concatenate(
            [
                lax.dot_general(
                    coupling[:, d * rank : (d + 1) * rank],
                    summed[d * rank : (d + 1) * rank, :],
                    TN,
                    precision=HIGHEST,
                    preferred_element_type=F32,
                )
                for d in range(LANES // rank)
            ],
            axis=0,
        ).T
        for part in split_bf(middle, 2):
            for h, panels in enumerate(halves):
                totals[h] = totals[h] + jnp.dot(part, panels[s][0:LANES], preferred_element_type=F32)
    for h, total in enumerate(totals):
        side = place[2] if h == 0 else 1 - place[2]
        for c in range(half // LANES):
            start = pl.multiple_of(side * half + c * LANES, LANES)
            out[pl.ds(start, LANES), :] = total[:, c * LANES : (c + 1) * LANES].T.astype(out.dtype)
    own = sent[0].shape[0] - rank
    for s in range(groups):
        owner = lax.rem(place[0] + s, groups)
        start = owner * (width // groups) + place[1] * own
        piece = start // cut
        turned[...] = sketches[piece].astype(F32).T
        sent[s][0:rank, :] = inverses
        sent[s][rank : rank + own, :] = turned[pl.ds(pl.multiple_of(start - piece * cut, 32), own), :]


def finish(place, parts, *refs):
    received, (left, right) = refs[:-2], refs[-2:]
    owners = len(received)
    groups = parts.shape[0] // owners
    targets = left.shape[0] // owners
    own, rank = left.shape[1], left.shape[2]
    root = math.sqrt(1024)
    for s in range(owners):
        owner = lax.rem(place[0] + owners - s, owners)
        total = parts[owner * groups].astype(F32)
        for z in range(1, groups):
            total = total + parts[owner * groups + z].astype(F32)
        both = jnp.concatenate([received[s][rank : rank + own, :] * root, total / root], axis=0)
        for t in range(targets):
            found = lax.dot_general(
                both[:, t * rank : (t + 1) * rank],
                received[s][0:rank, t * rank : (t + 1) * rank],
                NT,
                precision=HIGHEST,
                preferred_element_type=F32,
            )
            left[owner * targets + t] = found[0:own]
            right[owner * targets + t] = found[own : 2 * own]


def shards(sizes, entry_factor, entry_panel, entry_target, entry_count, panel_shared, coupling, probes):
    ny, nz, nx, nc = sizes
    y, z = lax.axis_index("y"), lax.axis_index("z")
    x, c = lax.axis_index("x"), lax.axis_index("core")
    place = jnp.stack([y, z, c]).astype(jnp.int32)
    factors = entry_factor[:, 0]
    slots, rank, width = factors.shape
    panels = panel_shared.shape[0]
    targets = probes.shape[0]
    rows = panels * rank
    mine = targets // ny
    own_rows = mine * rank
    held_rows = mine * panels * rank
    in_vmem = pl.BlockSpec(memory_space=VMEM)
    in_smem = pl.BlockSpec(memory_space=SMEM)
    in_any = pl.BlockSpec(memory_space=pl.ANY)

    def turn(value, axis, size, by):
        return lax.ppermute(value, axis, [(i, (i + by) % size) for i in range(size)])

    sums = pl.pallas_call(
        sum_factors,
        out_shape=(jax.ShapeDtypeStruct((held_rows, width), BF),) * ny,
        in_specs=[in_any] * 4,
        out_specs=(in_any,) * ny,
        scratch_shapes=[
            VMEM((slots, rank, width), BF),
            VMEM((targets * panels, rank, width), F32),
            VMEM((ny, held_rows, width), BF),
            SMEM((slots,), jnp.int32),
            SMEM((slots,), jnp.int32),
            SMEM((1,), jnp.int32),
            pltpu.SemaphoreType.DMA((6 + ny,)),
            pltpu.SemaphoreType.DMA((3,)),
        ],
        compiler_params=params(56),
        cost_estimate=pl.CostEstimate(flops=10**7, bytes_accessed=7 * 10**6, transcendentals=0),
        name="sum_factors",
    )(entry_panel[:, 0], entry_target[:, 0], entry_count[0], factors)
    held = [sums[0]] + [turn(sums[s], "y", ny, s) for s in range(1, ny)]

    own, _ = lax.optimization_barrier((panel_shared.reshape(rows, LANES), sums))
    pair = jnp.stack([own, turn(own, "core", nc, 1)])
    pieces = [pair] + [turn(pair, "x", nx, s) for s in range(1, nx)]
    columns = jnp.stack(
        [((x + nx - s) % nx) * nc + k for s in range(nx) for k in (c, (c + 1) % nc)] + [y, c]
    ).astype(jnp.int32)
    mine_half, other_half, *sent = pl.pallas_call(
        project,
        out_shape=(jax.ShapeDtypeStruct((rows + TAIL, width // 2), BF),) * 2
        + (jax.ShapeDtypeStruct((own_rows, rows), F32),)
        + (jax.ShapeDtypeStruct((own_rows, rows), BF),) * (ny - 1),
        in_specs=[in_smem] + [in_vmem] * (nx + 2),
        out_specs=(in_vmem,) * (ny + 2),
        scratch_shapes=[VMEM((rows + TAIL, width), BF), VMEM((targets * rank, rows), F32)],
        compiler_params=params(60),
        name="project",
    )(columns, *pieces, probes.reshape(targets * rank, width), coupling)
    coefficients = [sent[0].astype(BF)] + [turn(sent[s], "y", ny, s) for s in range(1, ny)]

    cut = width // nz
    sketch = pl.pallas_call(
        first_pass,
        out_shape=jax.ShapeDtypeStruct((nz, own_rows, cut), BF),
        in_specs=[in_vmem] * (2 * ny),
        out_specs=in_vmem,
        compiler_params=params(20),
        name="first_pass",
    )(*held, *coefficients)
    mine_half, sketch = lax.optimization_barrier((mine_half, sketch))
    near = [turn(mine_half, "y", ny, s) for s in (1, ny - 1)]
    parts = lax.all_to_all(sketch, "z", 0, 0, tiled=True)
    crossed = [turn(h, "core", nc, 1) for h in near]
    parts, near, crossed = lax.optimization_barrier((parts, near, crossed))
    far = [turn(near[0][:RELAY], "y", ny, 1), turn(near[1][RELAY:], "y", ny, ny - 1)]
    far_crossed = [turn(h, "core", nc, 1) for h in far]
    all_shared = [mine_half, near[0], *far, near[1], other_half, crossed[0], *far_crossed, crossed[1]]
    copies = pl.pallas_call(
        add_up,
        out_shape=jax.ShapeDtypeStruct((nz, own_rows, cut), BF),
        in_specs=[in_vmem],
        out_specs=in_vmem,
        compiler_params=params(8),
        name="add_up",
    )(parts)
    sketches = lax.all_to_all(copies, "z", 0, 0, tiled=True)

    keep = width // (ny * nz)
    rows_part, *sent = pl.pallas_call(
        second_pass,
        out_shape=(jax.ShapeDtypeStruct((width, own_rows), BF),)
        + (jax.ShapeDtypeStruct((rank + keep, own_rows), F32),) * ny,
        in_specs=[in_smem] + [in_vmem] * 15,
        out_specs=(in_vmem,) * (ny + 1),
        scratch_shapes=[VMEM((cut, own_rows), F32)],
        compiler_params=params(20),
        name="second_pass",
    )(place, sketches, *held, *all_shared)
    row_parts = lax.all_to_all(rows_part.reshape(ny * nz, keep, own_rows), ("y", "z"), 0, 0, tiled=True)
    received = [sent[0]] + [turn(sent[s], "y", ny, s) for s in range(1, ny)]
    out = jax.ShapeDtypeStruct((targets, keep, rank), F32)
    left_out, right_out = pl.pallas_call(
        finish,
        out_shape=(out, out),
        in_specs=[in_smem] + [in_vmem] * (ny + 1),
        out_specs=(in_vmem, in_vmem),
        compiler_params=params(8),
        name="finish",
    )(place, row_parts, *received)
    return left_out.transpose(0, 2, 1), right_out.transpose(0, 2, 1)


def solution(mesh):
    wide, narrow = mesh.devices.shape
    sizes = (4, wide // 4, narrow // 2, 2)
    axes = ("y", "z", "x", "core")
    finer = Mesh(mesh.devices.reshape(sizes), axes)
    split, owner = ("y", "z"), ("x", "core")
    placed = (
        P(split, owner, None, None),
        P(split, owner),
        P(split, owner),
        P(owner, split),
        P(split, None, owner),
        P(split, None, None),
        P(owner, None, None),
    )
    return jax.shard_map(
        functools.partial(shards, sizes),
        mesh=finer,
        in_specs=placed,
        out_specs=(P(owner, None, split), P(owner, None, split)),
        check_vma=False,
    )
```

```python
import functools
import math

import jax
import jax.numpy as jnp
from jax import lax
from jax.experimental import pallas as pl
from jax.experimental.pallas import tpu as pltpu
from jax.sharding import Mesh
from jax.sharding import PartitionSpec as P

BF = jnp.bfloat16
F32 = jnp.float32
HIGHEST = lax.Precision.HIGHEST
NT = (((1,), (1,)), ((), ()))
TN = (((0,), (0,)), ((), ()))
SMEM = pltpu.SMEM
VMEM = pltpu.VMEM
LANES = 128
BLOCK = 8
TAIL = 16
RELAY = 80


def params(mib):
    return pltpu.CompilerParams(vmem_limit_bytes=mib * 1024 * 1024)


def split_bf(x, parts):
    out = []
    for _ in range(parts):
        part = x.astype(BF)
        out.append(part)
        x = x - part.astype(F32)
    return out


def pack_rows(block):
    return jnp.concatenate([block[q * TAIL : (q + 1) * TAIL] for q in range(block.shape[0] // TAIL)], axis=1)


def unpack_rows(block):
    return jnp.concatenate([block[:, q * LANES : (q + 1) * LANES] for q in range(block.shape[1] // LANES)], axis=0)


def sum_factors(panel, target, count, factors, *refs):
    out, (loaded, acc, kept, panel_at, target_at, count_at, sems, small) = refs[:-8], refs[-8:]
    slots, rank, _ = loaded.shape
    pairs = acc.shape[0]
    panels = pairs // 8
    chunk = slots // 6
    indices = [
        pltpu.make_async_copy(source, to, small.at[i])
        for i, (source, to) in enumerate(((panel, panel_at), (target, target_at), (count, count_at)))
    ]
    for copy in indices:
        copy.start()
    loads = [
        pltpu.make_async_copy(factors.at[pl.ds(i * chunk, chunk)], loaded.at[pl.ds(i * chunk, chunk)], sems.at[i])
        for i in range(slots // chunk)
    ]
    for copy in loads:
        copy.start()

    def clear(i, _):
        acc[i] = jnp.zeros(acc.shape[1:], F32)
        return 0

    lax.fori_loop(0, pairs, clear, 0)
    for copy in indices:
        copy.wait()
    live = count_at[0]

    def add(e, _):
        pair = target_at[e] * panels + panel_at[e]
        acc[pair] += loaded[e].astype(F32)
        return 0

    for i, copy in enumerate(loads):
        copy.wait()
        lax.fori_loop(i * chunk, jnp.minimum(live, (i + 1) * chunk), add, 0)
    groups = len(out)
    each = pairs // groups
    here = lax.axis_index("y")
    stores = [pltpu.make_async_copy(kept.at[s - 1], out[s], sems.at[5 + s]) for s in range(1, groups)]
    direct = [
        pltpu.make_async_copy(acc.at[here * each + i], out[0].at[pl.ds(i * rank, rank)], sems.at[5 + groups + i])
        for i in range(each)
    ]
    for i in range(each):
        direct[i].start()
    for s in range(1, groups):
        owner = lax.rem(here + s, groups)
        for i in range(each):
            kept[s - 1, i * rank : (i + 1) * rank, :] = acc[owner * each + i].astype(BF)
        stores[s - 1].start()
    for copy in direct + stores:
        copy.wait()


def project(columns, *refs):
    pieces, refs = refs[:4], refs[4:]
    probes, coupling, mine, coefficients, shared = refs
    rows = pieces[0].shape[1]
    at = 0
    for piece in pieces:
        for half in range(piece.shape[0]):
            start = pl.multiple_of(columns[at] * LANES, LANES)
            shared[0:rows, pl.ds(start, LANES)] = piece[half]
            at += 1
    rank = coupling.shape[1]
    zero = jnp.zeros((rank, rank), F32)
    first, second = coupling[0], coupling[1]
    diagonal = jnp.concatenate(
        [jnp.concatenate([first, zero], axis=1), jnp.concatenate([zero, second], axis=1)], axis=0
    )
    projected = lax.dot_general(probes[...], shared[0:rows, :], NT, preferred_element_type=F32)
    found = lax.dot_general(projected, diagonal, NT, precision=HIGHEST, preferred_element_type=F32).astype(BF)
    each = coefficients.shape[1]
    for g in range(coefficients.shape[0]):
        coefficients[g] = found[g * each : (g + 1) * each]
    high, low = split_bf(jnp.concatenate([first, second], axis=1), 2)
    shared[rows : rows + TAIL, :] = jnp.concatenate([pack_rows(high), pack_rows(low)], axis=1)
    half = mine.shape[1]
    mine[...] = shared[:, pl.ds(pl.multiple_of(columns[at] * half, half), half)].astype(F32)


def first_pass(*refs):
    held, (coefficients, out) = refs[:-2], refs[-2:]
    groups = len(held)
    here = lax.axis_index("y")
    rows, width = held[0].shape
    targets = rows // LANES
    rank = out.shape[1] // targets
    cut = out.shape[2]
    totals = [jnp.zeros((rank, width), F32) for _ in range(targets)]
    for s in range(groups):
        source = lax.rem(here + groups - s, groups)
        for t in range(targets):
            totals[t] = totals[t] + jnp.dot(
                coefficients[source, t * rank : (t + 1) * rank, :],
                held[s][t * LANES : (t + 1) * LANES, :],
                preferred_element_type=F32,
            )
    for t in range(targets):
        for z in range(out.shape[0]):
            out[z, t * rank : (t + 1) * rank, :] = totals[t][:, z * cut : (z + 1) * cut].astype(BF)


def add_up(parts, out):
    total = parts[0].astype(F32)
    for z in range(1, parts.shape[0]):
        total = total + parts[z].astype(F32)
    for z in range(out.shape[0]):
        out[z] = total.astype(out.dtype)


def inverse_factors(grams):
    rank = grams[0].shape[0]
    row_at = lax.broadcasted_iota(jnp.int32, (rank, 2 * rank), 0)
    lane_at = lax.broadcasted_iota(jnp.int32, (rank, 2 * rank), 1)
    eye = (row_at + rank == lane_at).astype(F32)
    tables = [jnp.concatenate([g, jnp.zeros((rank, rank), F32)], axis=1) + eye for g in grams]
    for first in range(0, rank, BLOCK):
        top = (first // 8) * 8
        at = first - top
        for i, table in enumerate(tables):
            lower = table[top:, :]
            columns = [
                jnp.broadcast_to(lower[:, first + j : first + j + 1], lower.shape) for j in range(BLOCK)
            ]
            pivots = [lower[at + j : at + j + 1, :] for j in range(BLOCK)]
            for j in range(BLOCK):
                own = columns[j][at + j : at + j + 1, :]
                share = jnp.where(row_at[top:, :] > first + j, columns[j] * (1.0 / own), 0.0)
                for k in range(j + 1, BLOCK):
                    columns[k] = columns[k] - share * columns[j][at + k : at + k + 1, :]
                    pivots[k] = pivots[k] - share[at + k : at + k + 1, :] * pivots[j]
                lower = lower - share * pivots[j]
            tables[i] = lower if top == 0 else jnp.concatenate([table[:top], lower], axis=0)
    diagonal = row_at == lane_at
    return [
        (table * lax.rsqrt(jnp.sum(jnp.where(diagonal, table, 0.0), axis=1, keepdims=True)))[:, rank:]
        for table in tables
    ]


def second_pass(place, sketches, *refs):
    held, refs = refs[:4], refs[4:]
    groups = len(held)
    out, sent, (turned, kept, sems) = refs[10], refs[11:-3], refs[-3:]
    cuts, rows, cut = sketches.shape
    width = held[0].shape[1]
    targets = held[0].shape[0] // LANES
    rank = rows // targets
    whole = [
        jnp.concatenate([sketches[z, t * rank : (t + 1) * rank, :] for z in range(cuts)], axis=1)
        for t in range(targets)
    ]
    grams = [lax.dot_general(s, s, NT, preferred_element_type=F32) for s in whole]
    inverses = jnp.concatenate(inverse_factors(grams), axis=1)
    halves = [
        [
            refs[at][...],
            refs[at + 1][...],
            jnp.concatenate([refs[at + 2][...], refs[at + 3][...]], axis=0),
            refs[at + 4][...],
        ]
        for at in (0, 5)
    ]
    half = width // 2
    totals = [jnp.zeros((rows, half), F32) for _ in halves]
    for s in range(groups):
        summed = jnp.concatenate(
            [
                lax.dot_general(
                    held[s][t * LANES : (t + 1) * LANES, :], whole[t], NT, preferred_element_type=F32
                )
                for t in range(targets)
            ],
            axis=1,
        )
        coupling = unpack_rows(halves[0][s][LANES:]).astype(F32) + unpack_rows(halves[1][s][LANES:]).astype(F32)
        middle = jnp.concatenate(
            [
                lax.dot_general(
                    coupling[:, d * rank : (d + 1) * rank],
                    summed[d * rank : (d + 1) * rank, :],
                    TN,
                    precision=HIGHEST,
                    preferred_element_type=F32,
                )
                for d in range(LANES // rank)
            ],
            axis=0,
        ).T
        for part in split_bf(middle, 2):
            for h, panels in enumerate(halves):
                totals[h] = totals[h] + jnp.dot(part, panels[s][0:LANES], preferred_element_type=F32)
    for h, total in enumerate(totals):
        side = place[2] if h == 0 else 1 - place[2]
        for c in range(half // LANES):
            start = pl.multiple_of(side * half + c * LANES, LANES)
            out[pl.ds(start, LANES), :] = total[:, c * LANES : (c + 1) * LANES].T.astype(out.dtype)
    own = sent[0].shape[0] - rank
    for s in range(groups):
        owner = lax.rem(place[0] + s, groups)
        start = owner * (width // groups) + place[1] * own
        piece = start // cut
        turned[...] = sketches[piece].astype(F32).T
        kept[s, 0:rank, :] = inverses
        kept[s, rank : rank + own, :] = turned[pl.ds(pl.multiple_of(start - piece * cut, 32), own), :]
    copies = [pltpu.make_async_copy(kept.at[s], sent[s], sems.at[s]) for s in range(groups)]
    for copy in copies:
        copy.start()
    for copy in copies:
        copy.wait()


def finish(place, parts, *refs):
    received, (left, right) = refs[:-2], refs[-2:]
    owners = len(received)
    groups = parts.shape[0] // owners
    targets = left.shape[0] // owners
    own, rank = left.shape[1], left.shape[2]
    root = math.sqrt(1024)
    for s in range(owners):
        owner = lax.rem(place[0] + owners - s, owners)
        total = parts[owner * groups].astype(F32)
        for z in range(1, groups):
            total = total + parts[owner * groups + z].astype(F32)
        both = jnp.concatenate([received[s][rank : rank + own, :] * root, total / root], axis=0)
        for t in range(targets):
            found = lax.dot_general(
                both[:, t * rank : (t + 1) * rank],
                received[s][0:rank, t * rank : (t + 1) * rank],
                NT,
                precision=HIGHEST,
                preferred_element_type=F32,
            )
            left[owner * targets + t] = found[0:own]
            right[owner * targets + t] = found[own : 2 * own]


def shards(sizes, entry_factor, entry_panel, entry_target, entry_count, panel_shared, coupling, probes):
    ny, nz, nx, nc = sizes
    y, z = lax.axis_index("y"), lax.axis_index("z")
    x, c = lax.axis_index("x"), lax.axis_index("core")
    place = jnp.stack([y, z, c]).astype(jnp.int32)
    factors = entry_factor[:, 0]
    slots, rank, width = factors.shape
    panels = panel_shared.shape[0]
    targets = probes.shape[0]
    rows = panels * rank
    mine = targets // ny
    own_rows = mine * rank
    held_rows = mine * panels * rank
    in_vmem = pl.BlockSpec(memory_space=VMEM)
    in_smem = pl.BlockSpec(memory_space=SMEM)
    in_any = pl.BlockSpec(memory_space=pl.ANY)

    def turn(value, axis, size, by):
        return lax.ppermute(value, axis, [(i, (i + by) % size) for i in range(size)])

    sums = pl.pallas_call(
        sum_factors,
        out_shape=(jax.ShapeDtypeStruct((held_rows, width), F32),)
        + (jax.ShapeDtypeStruct((held_rows, width), BF),) * (ny - 1),
        in_specs=[in_any] * 4,
        out_specs=(in_any,) * ny,
        scratch_shapes=[
            VMEM((slots, rank, width), BF),
            VMEM((targets * panels, rank, width), F32),
            VMEM((ny - 1, held_rows, width), BF),
            SMEM((slots,), jnp.int32),
            SMEM((slots,), jnp.int32),
            SMEM((1,), jnp.int32),
            pltpu.SemaphoreType.DMA((5 + ny + mine * panels,)),
            pltpu.SemaphoreType.DMA((3,)),
        ],
        compiler_params=params(56),
        cost_estimate=pl.CostEstimate(flops=10**7, bytes_accessed=7 * 10**6, transcendentals=0),
        name="sum_factors",
    )(entry_panel[:, 0], entry_target[:, 0], entry_count[0], factors)
    held = [sums[0].astype(BF)] + [turn(sums[s], "y", ny, s) for s in range(1, ny)]

    own, _ = lax.optimization_barrier((panel_shared.reshape(rows, LANES), sums))
    pair = jnp.stack([own, turn(own, "core", nc, 1)])
    pieces = [pair] + [turn(pair, "x", nx, s) for s in range(1, nx)]
    columns = jnp.stack(
        [((x + nx - s) % nx) * nc + k for s in range(nx) for k in (c, (c + 1) % nc)] + [c]
    ).astype(jnp.int32)
    mine_half, found = pl.pallas_call(
        project,
        out_shape=(
            jax.ShapeDtypeStruct((rows + TAIL, width // 2), F32),
            jax.ShapeDtypeStruct((ny, own_rows, rows), BF),
        ),
        in_specs=[in_smem] + [in_vmem] * (nx + 2),
        out_specs=(in_vmem,) * 2,
        scratch_shapes=[VMEM((rows + TAIL, width), BF)],
        compiler_params=params(60),
        name="project",
    )(columns, *pieces, probes.reshape(targets * rank, width), coupling)
    coefficients = lax.all_to_all(found, "y", 0, 0, tiled=True)
    mine_half = mine_half.astype(BF)

    cut = width // nz
    sketch = pl.pallas_call(
        first_pass,
        out_shape=jax.ShapeDtypeStruct((nz, own_rows, cut), BF),
        in_specs=[in_vmem] * (ny + 1),
        out_specs=in_vmem,
        compiler_params=params(20),
        name="first_pass",
    )(*held, coefficients)
    mine_half, sketch = lax.optimization_barrier((mine_half, sketch))
    near = [turn(mine_half, "y", ny, s) for s in (1, ny - 1)]
    parts = lax.all_to_all(sketch, "z", 0, 0, tiled=True)
    other_half = turn(mine_half, "core", nc, 1)
    parts, near, other_half = lax.optimization_barrier((parts, near, other_half))
    far = [turn(near[0][:RELAY], "y", ny, 1), turn(near[1][RELAY:], "y", ny, ny - 1)]
    near, far = lax.optimization_barrier((near, far))
    halves = [near[0], *far, near[1]]
    all_shared = [mine_half, *halves, other_half] + [turn(h, "core", nc, 1) for h in halves]
    copies = pl.pallas_call(
        add_up,
        out_shape=jax.ShapeDtypeStruct((nz, own_rows, cut), BF),
        in_specs=[in_vmem],
        out_specs=in_vmem,
        compiler_params=params(8),
        name="add_up",
    )(parts)
    sketches = lax.all_to_all(copies, "z", 0, 0, tiled=True)

    keep = width // (ny * nz)
    rows_part, *sent = pl.pallas_call(
        second_pass,
        out_shape=(jax.ShapeDtypeStruct((width, own_rows), BF),)
        + (pltpu.HBM((rank + keep, own_rows), F32),) * ny,
        in_specs=[in_smem] + [in_vmem] * 15,
        out_specs=(in_vmem,) + (pl.BlockSpec(memory_space=pltpu.HBM),) * ny,
        scratch_shapes=[
            VMEM((cut, own_rows), F32),
            VMEM((ny, rank + keep, own_rows), F32),
            pltpu.SemaphoreType.DMA((ny,)),
        ],
        compiler_params=params(20),
        name="second_pass",
    )(place, sketches, *held, *all_shared)
    row_parts = lax.all_to_all(rows_part.reshape(ny * nz, keep, own_rows), ("y", "z"), 0, 0, tiled=True)
    received = [sent[0]] + [turn(sent[s], "y", ny, s) for s in range(1, ny)]
    out = jax.ShapeDtypeStruct((targets, keep, rank), F32)
    left_out, right_out = pl.pallas_call(
        finish,
        out_shape=(out, out),
        in_specs=[in_smem] + [in_vmem] * (ny + 1),
        out_specs=(in_vmem, in_vmem),
        compiler_params=params(8),
        name="finish",
    )(place, row_parts, *received)
    return left_out.transpose(0, 2, 1), right_out.transpose(0, 2, 1)


def solution(mesh):
    wide, narrow = mesh.devices.shape
    sizes = (4, wide // 4, narrow // 2, 2)
    axes = ("y", "z", "x", "core")
    finer = Mesh(mesh.devices.reshape(sizes), axes)
    split, owner = ("y", "z"), ("x", "core")
    placed = (
        P(split, owner, None, None),
        P(split, owner),
        P(split, owner),
        P(owner, split),
        P(split, None, owner),
        P(split, None, None),
        P(owner, None, None),
    )
    return jax.shard_map(
        functools.partial(shards, sizes),
        mesh=finer,
        in_specs=placed,
        out_specs=(P(owner, None, split), P(owner, None, split)),
        check_vma=False,
    )
```

```python
import functools
import math

import jax
import jax.numpy as jnp
from jax import lax
from jax.experimental import pallas as pl
from jax.experimental.pallas import tpu as pltpu
from jax.sharding import Mesh
from jax.sharding import PartitionSpec as P

BF = jnp.bfloat16
F32 = jnp.float32
HIGHEST = lax.Precision.HIGHEST
NT = (((1,), (1,)), ((), ()))
TN = (((0,), (0,)), ((), ()))
SMEM = pltpu.SMEM
VMEM = pltpu.VMEM
LANES = 128
BLOCK = 8
TAIL = 16
RELAY = 80


def params(mib):
    return pltpu.CompilerParams(vmem_limit_bytes=mib * 1024 * 1024)


def split_bf(x, parts):
    out = []
    for _ in range(parts):
        part = x.astype(BF)
        out.append(part)
        x = x - part.astype(F32)
    return out


def pack_rows(block):
    return jnp.concatenate([block[q * TAIL : (q + 1) * TAIL] for q in range(block.shape[0] // TAIL)], axis=1)


def unpack_rows(block):
    return jnp.concatenate([block[:, q * LANES : (q + 1) * LANES] for q in range(block.shape[1] // LANES)], axis=0)


def sum_factors(panel, target, count, factors, *refs):
    out, (loaded, acc, kept, panel_at, target_at, count_at, sems, small) = refs[:-8], refs[-8:]
    slots, rank, _ = loaded.shape
    pairs = acc.shape[0]
    panels = pairs // 8
    chunk = slots // 6
    indices = [
        pltpu.make_async_copy(source, to, small.at[i])
        for i, (source, to) in enumerate(((panel, panel_at), (target, target_at), (count, count_at)))
    ]
    for copy in indices:
        copy.start()
    loads = [
        pltpu.make_async_copy(factors.at[pl.ds(i * chunk, chunk)], loaded.at[pl.ds(i * chunk, chunk)], sems.at[i])
        for i in range(slots // chunk)
    ]
    for copy in loads:
        copy.start()

    def clear(i, _):
        acc[i] = jnp.zeros(acc.shape[1:], F32)
        return 0

    lax.fori_loop(0, pairs, clear, 0)
    for copy in indices:
        copy.wait()
    live = count_at[0]

    def add(e, _):
        pair = target_at[e] * panels + panel_at[e]
        acc[pair] += loaded[e].astype(F32)
        return 0

    for i, copy in enumerate(loads):
        copy.wait()
        lax.fori_loop(i * chunk, jnp.minimum(live, (i + 1) * chunk), add, 0)
    groups = len(out)
    each = pairs // groups
    here = lax.axis_index("y")
    stores = [pltpu.make_async_copy(kept.at[s - 1], out[s], sems.at[5 + s]) for s in range(1, groups)]
    direct = [
        pltpu.make_async_copy(acc.at[here * each + i], out[0].at[pl.ds(i * rank, rank)], sems.at[5 + groups + i])
        for i in range(each)
    ]
    for i in range(each):
        direct[i].start()
    for s in range(1, groups):
        owner = lax.rem(here + s, groups)
        for i in range(each):
            kept[s - 1, i * rank : (i + 1) * rank, :] = acc[owner * each + i].astype(BF)
        stores[s - 1].start()
    for copy in direct + stores:
        copy.wait()


def project(columns, *refs):
    pieces, refs = refs[:4], refs[4:]
    probes, coupling, mine, coefficients, shared = refs
    rows = pieces[0].shape[1]
    at = 0
    for piece in pieces:
        for half in range(piece.shape[0]):
            start = pl.multiple_of(columns[at] * LANES, LANES)
            shared[0:rows, pl.ds(start, LANES)] = piece[half]
            at += 1
    rank = coupling.shape[1]
    zero = jnp.zeros((rank, rank), F32)
    first, second = coupling[0], coupling[1]
    diagonal = jnp.concatenate(
        [jnp.concatenate([first, zero], axis=1), jnp.concatenate([zero, second], axis=1)], axis=0
    )
    projected = lax.dot_general(probes[...], shared[0:rows, :], NT, preferred_element_type=F32)
    found = lax.dot_general(projected, diagonal, NT, precision=HIGHEST, preferred_element_type=F32).astype(BF)
    each = coefficients.shape[1]
    for g in range(coefficients.shape[0]):
        coefficients[g] = found[g * each : (g + 1) * each]
    high, low = split_bf(jnp.concatenate([first, second], axis=1), 2)
    shared[rows : rows + TAIL, :] = jnp.concatenate([pack_rows(high), pack_rows(low)], axis=1)
    half = mine.shape[1]
    mine[...] = shared[:, pl.ds(pl.multiple_of(columns[at] * half, half), half)].astype(F32)


def first_pass(*refs):
    held, (coefficients, out) = refs[:-2], refs[-2:]
    groups = len(held)
    here = lax.axis_index("y")
    rows, width = held[0].shape
    targets = rows // LANES
    rank = out.shape[1] // targets
    cut = out.shape[2]
    totals = [jnp.zeros((rank, width), F32) for _ in range(targets)]
    for s in range(groups):
        source = lax.rem(here + groups - s, groups)
        for t in range(targets):
            totals[t] = totals[t] + jnp.dot(
                coefficients[source, t * rank : (t + 1) * rank, :],
                held[s][t * LANES : (t + 1) * LANES, :],
                preferred_element_type=F32,
            )
    for t in range(targets):
        for z in range(out.shape[0]):
            out[z, t * rank : (t + 1) * rank, :] = totals[t][:, z * cut : (z + 1) * cut].astype(BF)


def add_up(parts, out):
    total = parts[0].astype(F32)
    for z in range(1, parts.shape[0]):
        total = total + parts[z].astype(F32)
    for z in range(out.shape[0]):
        out[z] = total.astype(out.dtype)


def inverse_factors(grams):
    rank = grams[0].shape[0]
    row_at = lax.broadcasted_iota(jnp.int32, (rank, 2 * rank), 0)
    lane_at = lax.broadcasted_iota(jnp.int32, (rank, 2 * rank), 1)
    eye = (row_at + rank == lane_at).astype(F32)
    tables = [jnp.concatenate([g, jnp.zeros((rank, rank), F32)], axis=1) + eye for g in grams]
    for first in range(0, rank, BLOCK):
        top = (first // 8) * 8
        at = first - top
        for i, table in enumerate(tables):
            lower = table[top:, :]
            columns = [
                jnp.broadcast_to(lower[:, first + j : first + j + 1], lower.shape) for j in range(BLOCK)
            ]
            pivots = [lower[at + j : at + j + 1, :] for j in range(BLOCK)]
            for j in range(BLOCK):
                own = columns[j][at + j : at + j + 1, :]
                share = jnp.where(row_at[top:, :] > first + j, columns[j] * (1.0 / own), 0.0)
                for k in range(j + 1, BLOCK):
                    columns[k] = columns[k] - share * columns[j][at + k : at + k + 1, :]
                    pivots[k] = pivots[k] - share[at + k : at + k + 1, :] * pivots[j]
                lower = lower - share * pivots[j]
            tables[i] = lower if top == 0 else jnp.concatenate([table[:top], lower], axis=0)
    diagonal = row_at == lane_at
    return [
        (table * lax.rsqrt(jnp.sum(jnp.where(diagonal, table, 0.0), axis=1, keepdims=True)))[:, rank:]
        for table in tables
    ]


def second_pass(place, sketches, *refs):
    held, refs = refs[:4], refs[4:]
    groups = len(held)
    out, sent, (turned, kept, sems) = refs[10], refs[11:-3], refs[-3:]
    cuts, rows, cut = sketches.shape
    width = held[0].shape[1]
    targets = held[0].shape[0] // LANES
    rank = rows // targets
    whole = [
        jnp.concatenate([sketches[z, t * rank : (t + 1) * rank, :] for z in range(cuts)], axis=1)
        for t in range(targets)
    ]
    grams = [lax.dot_general(s, s, NT, preferred_element_type=F32) for s in whole]
    inverses = jnp.concatenate(inverse_factors(grams), axis=1)
    halves = [
        [
            refs[at][...],
            refs[at + 1][...],
            jnp.concatenate([refs[at + 2][...], refs[at + 3][...]], axis=0),
            refs[at + 4][...],
        ]
        for at in (0, 5)
    ]
    half = width // 2
    own = sent[0].shape[0] - rank
    totals = [jnp.zeros((rows, half), F32) for _ in halves]
    for s in range(groups):
        summed = jnp.concatenate(
            [
                lax.dot_general(
                    held[s][t * LANES : (t + 1) * LANES, :], whole[t], NT, preferred_element_type=F32
                )
                for t in range(targets)
            ],
            axis=1,
        )
        coupling = unpack_rows(halves[0][s][LANES:]).astype(F32) + unpack_rows(halves[1][s][LANES:]).astype(F32)
        middle = jnp.concatenate(
            [
                lax.dot_general(
                    coupling[:, d * rank : (d + 1) * rank],
                    summed[d * rank : (d + 1) * rank, :],
                    TN,
                    precision=HIGHEST,
                    preferred_element_type=F32,
                )
                for d in range(LANES // rank)
            ],
            axis=0,
        ).T
        for part in split_bf(middle, 2):
            for h, panels in enumerate(halves):
                totals[h] = totals[h] + jnp.dot(part, panels[s][0:LANES], preferred_element_type=F32)
    for h, total in enumerate(totals):
        side = place[2] if h == 0 else 1 - place[2]
        for c in range(half // LANES):
            block = total[:, c * LANES : (c + 1) * LANES].T.astype(out.dtype)
            first = side * (half // own) + c * (LANES // own)
            for k in range(LANES // own):
                to = lax.rem(first + k, cuts) * groups + (first + k) // cuts
                out[pl.ds(pl.multiple_of(to * own, own), own), :] = block[k * own : (k + 1) * own]
    for s in range(groups):
        owner = lax.rem(place[0] + s, groups)
        start = owner * (width // groups) + place[1] * own
        piece = start // cut
        turned[...] = sketches[piece].astype(F32).T
        kept[s, 0:rank, :] = inverses
        kept[s, rank : rank + own, :] = turned[pl.ds(pl.multiple_of(start - piece * cut, 32), own), :]
    copies = [pltpu.make_async_copy(kept.at[s], sent[s], sems.at[s]) for s in range(groups)]
    for copy in copies:
        copy.start()
    for copy in copies:
        copy.wait()


def finish(place, parts, own_far, *refs):
    received, (left, right, own_near, sem) = refs[:-4], refs[-4:]
    copy = pltpu.make_async_copy(own_far, own_near, sem)
    copy.start()
    received = [own_near, *received]
    owners = len(received)
    groups = parts.shape[0] // owners
    targets = left.shape[0] // owners
    own, rank = left.shape[1], left.shape[2]
    root = math.sqrt(1024)
    for s in [*range(1, owners), 0]:
        if s == 0:
            copy.wait()
        owner = lax.rem(place[0] + owners - s, owners)
        total = parts[owner].astype(F32)
        for z in range(1, groups):
            total = total + parts[z * owners + owner].astype(F32)
        both = jnp.concatenate([received[s][rank : rank + own, :] * root, total / root], axis=0)
        for t in range(targets):
            found = lax.dot_general(
                both[:, t * rank : (t + 1) * rank],
                received[s][0:rank, t * rank : (t + 1) * rank],
                NT,
                precision=HIGHEST,
                preferred_element_type=F32,
            )
            left[owner * targets + t] = found[0:own]
            right[owner * targets + t] = found[own : 2 * own]


def shards(sizes, entry_factor, entry_panel, entry_target, entry_count, panel_shared, coupling, probes):
    ny, nz, nx, nc = sizes
    y, z = lax.axis_index("y"), lax.axis_index("z")
    x, c = lax.axis_index("x"), lax.axis_index("core")
    place = jnp.stack([y, z, c]).astype(jnp.int32)
    factors = entry_factor[:, 0]
    slots, rank, width = factors.shape
    panels = panel_shared.shape[0]
    targets = probes.shape[0]
    rows = panels * rank
    mine = targets // ny
    own_rows = mine * rank
    held_rows = mine * panels * rank
    in_vmem = pl.BlockSpec(memory_space=VMEM)
    in_smem = pl.BlockSpec(memory_space=SMEM)
    in_any = pl.BlockSpec(memory_space=pl.ANY)

    def turn(value, axis, size, by):
        return lax.ppermute(value, axis, [(i, (i + by) % size) for i in range(size)])

    sums = pl.pallas_call(
        sum_factors,
        out_shape=(jax.ShapeDtypeStruct((held_rows, width), F32),)
        + (jax.ShapeDtypeStruct((held_rows, width), BF),) * (ny - 1),
        in_specs=[in_any] * 4,
        out_specs=(in_any,) * ny,
        scratch_shapes=[
            VMEM((slots, rank, width), BF),
            VMEM((targets * panels, rank, width), F32),
            VMEM((ny - 1, held_rows, width), BF),
            SMEM((slots,), jnp.int32),
            SMEM((slots,), jnp.int32),
            SMEM((1,), jnp.int32),
            pltpu.SemaphoreType.DMA((5 + ny + mine * panels,)),
            pltpu.SemaphoreType.DMA((3,)),
        ],
        compiler_params=params(56),
        cost_estimate=pl.CostEstimate(flops=10**7, bytes_accessed=7 * 10**6, transcendentals=0),
        name="sum_factors",
    )(entry_panel[:, 0], entry_target[:, 0], entry_count[0], factors)
    held = [sums[0].astype(BF)] + [turn(sums[s], "y", ny, s) for s in range(1, ny)]

    own, _ = lax.optimization_barrier((panel_shared.reshape(rows, LANES), sums))
    pair = jnp.stack([own, turn(own, "core", nc, 1)])
    pieces = [pair] + [turn(pair, "x", nx, s) for s in range(1, nx)]
    columns = jnp.stack(
        [((x + nx - s) % nx) * nc + k for s in range(nx) for k in (c, (c + 1) % nc)] + [c]
    ).astype(jnp.int32)
    mine_half, found = pl.pallas_call(
        project,
        out_shape=(
            jax.ShapeDtypeStruct((rows + TAIL, width // 2), F32),
            jax.ShapeDtypeStruct((ny, own_rows, rows), BF),
        ),
        in_specs=[in_smem] + [in_vmem] * (nx + 2),
        out_specs=(in_vmem,) * 2,
        scratch_shapes=[VMEM((rows + TAIL, width), BF)],
        compiler_params=params(60),
        name="project",
    )(columns, *pieces, probes.reshape(targets * rank, width), coupling)
    coefficients = lax.all_to_all(found, "y", 0, 0, tiled=True)
    mine_half = mine_half.astype(BF)

    cut = width // nz
    sketch = pl.pallas_call(
        first_pass,
        out_shape=jax.ShapeDtypeStruct((nz, own_rows, cut), BF),
        in_specs=[in_vmem] * (ny + 1),
        out_specs=in_vmem,
        compiler_params=params(20),
        name="first_pass",
    )(*held, coefficients)
    mine_half, sketch = lax.optimization_barrier((mine_half, sketch))
    near = [turn(mine_half, "y", ny, s) for s in (1, ny - 1)]
    parts = lax.all_to_all(sketch, "z", 0, 0, tiled=True)
    other_half = turn(mine_half, "core", nc, 1)
    parts, near, other_half = lax.optimization_barrier((parts, near, other_half))
    far = [turn(near[0][:RELAY], "y", ny, 1), turn(near[1][RELAY:], "y", ny, ny - 1)]
    near, far = lax.optimization_barrier((near, far))
    halves = [near[0], *far, near[1]]
    all_shared = [mine_half, *halves, other_half] + [turn(h, "core", nc, 1) for h in halves]
    copies = pl.pallas_call(
        add_up,
        out_shape=jax.ShapeDtypeStruct((nz, own_rows, cut), BF),
        in_specs=[in_vmem],
        out_specs=in_vmem,
        compiler_params=params(8),
        name="add_up",
    )(parts)
    sketches = lax.all_to_all(copies, "z", 0, 0, tiled=True)

    keep = width // (ny * nz)
    rows_part, *sent = pl.pallas_call(
        second_pass,
        out_shape=(jax.ShapeDtypeStruct((width, own_rows), BF),)
        + (pltpu.HBM((rank + keep, own_rows), F32),) * ny,
        in_specs=[in_smem] + [in_vmem] * 15,
        out_specs=(in_vmem,) + (pl.BlockSpec(memory_space=pltpu.HBM),) * ny,
        scratch_shapes=[
            VMEM((cut, own_rows), F32),
            VMEM((ny, rank + keep, own_rows), F32),
            pltpu.SemaphoreType.DMA((ny,)),
        ],
        compiler_params=params(20),
        name="second_pass",
    )(place, sketches, *held, *all_shared)
    row_parts = lax.all_to_all(rows_part.reshape(ny * nz, keep, own_rows), ("z", "y"), 0, 0, tiled=True)
    received = [pltpu.with_memory_space_constraint(sent[0], pltpu.HBM)] + [turn(sent[s], "y", ny, s) for s in range(1, ny)]
    out = jax.ShapeDtypeStruct((targets, keep, rank), F32)
    left_out, right_out = pl.pallas_call(
        finish,
        out_shape=(out, out),
        in_specs=[in_smem, in_vmem, pl.BlockSpec(memory_space=pltpu.HBM)] + [in_vmem] * (ny - 1),
        out_specs=(in_vmem, in_vmem),
        scratch_shapes=[VMEM((rank + keep, own_rows), F32), pltpu.SemaphoreType.DMA],
        compiler_params=params(8),
        name="finish",
    )(place, row_parts, *received)
    return left_out.transpose(0, 2, 1), right_out.transpose(0, 2, 1)


def solution(mesh):
    wide, narrow = mesh.devices.shape
    sizes = (4, wide // 4, narrow // 2, 2)
    axes = ("y", "z", "x", "core")
    finer = Mesh(mesh.devices.reshape(sizes), axes)
    split, owner = ("y", "z"), ("x", "core")
    placed = (
        P(split, owner, None, None),
        P(split, owner),
        P(split, owner),
        P(owner, split),
        P(split, None, owner),
        P(split, None, None),
        P(owner, None, None),
    )
    return jax.shard_map(
        functools.partial(shards, sizes),
        mesh=finer,
        in_specs=placed,
        out_specs=(P(owner, None, split), P(owner, None, split)),
        check_vma=False,
    )
```

```python
import functools
import math

import jax
import jax.numpy as jnp
from jax import lax
from jax.experimental import pallas as pl
from jax.experimental.pallas import tpu as pltpu
from jax.sharding import Mesh
from jax.sharding import PartitionSpec as P

BF = jnp.bfloat16
F32 = jnp.float32
HIGHEST = lax.Precision.HIGHEST
NT = (((1,), (1,)), ((), ()))
TN = (((0,), (0,)), ((), ()))
SMEM = pltpu.SMEM
VMEM = pltpu.VMEM
LANES = 128
BLOCK = 8
TAIL = 16
RELAY = 80


def params(mib):
    return pltpu.CompilerParams(vmem_limit_bytes=mib * 1024 * 1024)


def split_bf(x, parts):
    out = []
    for _ in range(parts):
        part = x.astype(BF)
        out.append(part)
        x = x - part.astype(F32)
    return out


def pack_rows(block):
    return jnp.concatenate([block[q * TAIL : (q + 1) * TAIL] for q in range(block.shape[0] // TAIL)], axis=1)


def unpack_rows(block):
    return jnp.concatenate([block[:, q * LANES : (q + 1) * LANES] for q in range(block.shape[1] // LANES)], axis=0)


def sum_factors(panel, target, count, factors, *refs):
    out, (loaded, acc, kept, panel_at, target_at, count_at, sems, small) = refs[:-8], refs[-8:]
    slots, rank, _ = loaded.shape
    pairs = acc.shape[0]
    panels = pairs // 8
    chunk = slots // 6
    indices = [
        pltpu.make_async_copy(source, to, small.at[i])
        for i, (source, to) in enumerate(((panel, panel_at), (target, target_at), (count, count_at)))
    ]
    for copy in indices:
        copy.start()
    loads = [
        pltpu.make_async_copy(factors.at[pl.ds(i * chunk, chunk)], loaded.at[pl.ds(i * chunk, chunk)], sems.at[i])
        for i in range(slots // chunk)
    ]
    for copy in loads:
        copy.start()

    def clear(i, _):
        acc[i] = jnp.zeros(acc.shape[1:], F32)
        return 0

    lax.fori_loop(0, pairs, clear, 0)
    for copy in indices:
        copy.wait()
    live = count_at[0]

    def add(e, _):
        pair = target_at[e] * panels + panel_at[e]
        acc[pair] += loaded[e].astype(F32)
        return 0

    for i, copy in enumerate(loads):
        copy.wait()
        lax.fori_loop(i * chunk, jnp.minimum(live, (i + 1) * chunk), add, 0)
    groups = len(out)
    each = pairs // groups
    here = lax.axis_index("y")
    stores = [pltpu.make_async_copy(kept.at[s - 1], out[s], sems.at[5 + s]) for s in range(1, groups)]
    direct = [
        pltpu.make_async_copy(acc.at[here * each + i], out[0].at[pl.ds(i * rank, rank)], sems.at[5 + groups + i])
        for i in range(each)
    ]
    for i in range(each):
        direct[i].start()
    for s in range(1, groups):
        owner = lax.rem(here + s, groups)
        for i in range(each):
            kept[s - 1, i * rank : (i + 1) * rank, :] = acc[owner * each + i].astype(BF)
        stores[s - 1].start()
    for copy in direct + stores:
        copy.wait()


def project(columns, *refs):
    pieces, refs = refs[:4], refs[4:]
    probes, coupling, mine, coefficients, shared = refs
    rows = pieces[0].shape[1]
    at = 0
    for piece in pieces:
        for half in range(piece.shape[0]):
            start = pl.multiple_of(columns[at] * LANES, LANES)
            shared[0:rows, pl.ds(start, LANES)] = piece[half]
            at += 1
    rank = coupling.shape[1]
    zero = jnp.zeros((rank, rank), F32)
    first, second = coupling[0], coupling[1]
    diagonal = jnp.concatenate(
        [jnp.concatenate([first, zero], axis=1), jnp.concatenate([zero, second], axis=1)], axis=0
    )
    projected = lax.dot_general(probes[...], shared[0:rows, :], NT, preferred_element_type=F32)
    found = lax.dot_general(projected, diagonal, NT, precision=HIGHEST, preferred_element_type=F32).astype(BF)
    each = coefficients.shape[1]
    for g in range(coefficients.shape[0]):
        coefficients[g] = found[g * each : (g + 1) * each]
    high, low = split_bf(jnp.concatenate([first, second], axis=1), 2)
    shared[rows : rows + TAIL, :] = jnp.concatenate([pack_rows(high), pack_rows(low)], axis=1)
    mine[...] = shared[...].astype(F32)


def first_pass(*refs):
    held, (coefficients, out) = refs[:-2], refs[-2:]
    groups = len(held)
    here = lax.axis_index("y")
    rows, width = held[0].shape
    targets = rows // LANES
    rank = out.shape[1] // targets
    cut = out.shape[2]
    totals = [jnp.zeros((rank, width), F32) for _ in range(targets)]
    for s in range(groups):
        source = lax.rem(here + groups - s, groups)
        for t in range(targets):
            totals[t] = totals[t] + jnp.dot(
                coefficients[source, t * rank : (t + 1) * rank, :],
                held[s][t * LANES : (t + 1) * LANES, :],
                preferred_element_type=F32,
            )
    for t in range(targets):
        for z in range(out.shape[0]):
            out[z, t * rank : (t + 1) * rank, :] = totals[t][:, z * cut : (z + 1) * cut].astype(BF)


def add_up(parts, out):
    total = parts[0].astype(F32)
    for z in range(1, parts.shape[0]):
        total = total + parts[z].astype(F32)
    for z in range(out.shape[0]):
        out[z] = total.astype(out.dtype)


def inverse_factors(grams):
    rank = grams[0].shape[0]
    row_at = lax.broadcasted_iota(jnp.int32, (rank, 2 * rank), 0)
    lane_at = lax.broadcasted_iota(jnp.int32, (rank, 2 * rank), 1)
    eye = (row_at + rank == lane_at).astype(F32)
    tables = [jnp.concatenate([g, jnp.zeros((rank, rank), F32)], axis=1) + eye for g in grams]
    for first in range(0, rank, BLOCK):
        top = (first // 8) * 8
        at = first - top
        for i, table in enumerate(tables):
            lower = table[top:, :]
            columns = [
                jnp.broadcast_to(lower[:, first + j : first + j + 1], lower.shape) for j in range(BLOCK)
            ]
            pivots = [lower[at + j : at + j + 1, :] for j in range(BLOCK)]
            for j in range(BLOCK):
                own = columns[j][at + j : at + j + 1, :]
                share = jnp.where(row_at[top:, :] > first + j, columns[j] * (1.0 / own), 0.0)
                for k in range(j + 1, BLOCK):
                    columns[k] = columns[k] - share * columns[j][at + k : at + k + 1, :]
                    pivots[k] = pivots[k] - share[at + k : at + k + 1, :] * pivots[j]
                lower = lower - share * pivots[j]
            tables[i] = lower if top == 0 else jnp.concatenate([table[:top], lower], axis=0)
    diagonal = row_at == lane_at
    return [
        (table * lax.rsqrt(jnp.sum(jnp.where(diagonal, table, 0.0), axis=1, keepdims=True)))[:, rank:]
        for table in tables
    ]


def second_pass(place, sketches, *refs):
    held, refs = refs[:4], refs[4:]
    groups = len(held)
    out, sent, (turned, kept, sems) = refs[5], refs[6:-3], refs[-3:]
    cuts, rows, cut = sketches.shape
    width = held[0].shape[1]
    targets = held[0].shape[0] // LANES
    rank = rows // targets
    whole = [
        jnp.concatenate([sketches[z, t * rank : (t + 1) * rank, :] for z in range(cuts)], axis=1)
        for t in range(targets)
    ]
    grams = [lax.dot_general(s, s, NT, preferred_element_type=F32) for s in whole]
    inverses = jnp.concatenate(inverse_factors(grams), axis=1)
    panels = [refs[0][...], refs[1][...], jnp.concatenate([refs[2][...], refs[3][...]], axis=0), refs[4][...]]
    half = width // 2
    own = sent[0].shape[0] - rank
    total = jnp.zeros((rows, width), F32)
    for s in range(groups):
        summed = jnp.concatenate(
            [
                lax.dot_general(
                    held[s][t * LANES : (t + 1) * LANES, :], whole[t], NT, preferred_element_type=F32
                )
                for t in range(targets)
            ],
            axis=1,
        )
        coupling = unpack_rows(panels[s][LANES:, :half]).astype(F32) + unpack_rows(panels[s][LANES:, half:]).astype(F32)
        middle = jnp.concatenate(
            [
                lax.dot_general(
                    coupling[:, d * rank : (d + 1) * rank],
                    summed[d * rank : (d + 1) * rank, :],
                    TN,
                    precision=HIGHEST,
                    preferred_element_type=F32,
                )
                for d in range(LANES // rank)
            ],
            axis=0,
        ).T
        for part in split_bf(middle, 2):
            total = total + jnp.dot(part, panels[s][0:LANES], preferred_element_type=F32)
    for c in range(width // LANES):
        block = total[:, c * LANES : (c + 1) * LANES].T.astype(out.dtype)
        for k in range(LANES // own):
            first = c * (LANES // own) + k
            to = (first % cuts) * groups + first // cuts
            out[to * own : (to + 1) * own, :] = block[k * own : (k + 1) * own]
    for s in range(groups):
        owner = lax.rem(place[0] + s, groups)
        start = owner * (width // groups) + place[1] * own
        piece = start // cut
        turned[...] = sketches[piece].astype(F32).T
        kept[s, 0:rank, :] = inverses
        kept[s, rank : rank + own, :] = turned[pl.ds(pl.multiple_of(start - piece * cut, 32), own), :]
    copies = [pltpu.make_async_copy(kept.at[s], sent[s], sems.at[s]) for s in range(groups)]
    for copy in copies:
        copy.start()
    for copy in copies:
        copy.wait()


def finish(place, parts, own_far, *refs):
    received, (left, right, own_near, sem) = refs[:-4], refs[-4:]
    copy = pltpu.make_async_copy(own_far, own_near, sem)
    copy.start()
    received = [own_near, *received]
    owners = len(received)
    groups = parts.shape[0] // owners
    targets = left.shape[0] // owners
    own, rank = left.shape[1], left.shape[2]
    root = math.sqrt(1024)
    for s in [*range(1, owners), 0]:
        if s == 0:
            copy.wait()
        owner = lax.rem(place[0] + owners - s, owners)
        total = parts[owner].astype(F32)
        for z in range(1, groups):
            total = total + parts[z * owners + owner].astype(F32)
        both = jnp.concatenate([received[s][rank : rank + own, :] * root, total / root], axis=0)
        for t in range(targets):
            found = lax.dot_general(
                both[:, t * rank : (t + 1) * rank],
                received[s][0:rank, t * rank : (t + 1) * rank],
                NT,
                precision=HIGHEST,
                preferred_element_type=F32,
            )
            left[owner * targets + t] = found[0:own]
            right[owner * targets + t] = found[own : 2 * own]


def shards(sizes, entry_factor, entry_panel, entry_target, entry_count, panel_shared, coupling, probes):
    ny, nz, nx, nc = sizes
    y, z = lax.axis_index("y"), lax.axis_index("z")
    x, c = lax.axis_index("x"), lax.axis_index("core")
    place = jnp.stack([y, z, c]).astype(jnp.int32)
    factors = entry_factor[:, 0]
    slots, rank, width = factors.shape
    panels = panel_shared.shape[0]
    targets = probes.shape[0]
    rows = panels * rank
    mine = targets // ny
    own_rows = mine * rank
    held_rows = mine * panels * rank
    in_vmem = pl.BlockSpec(memory_space=VMEM)
    in_smem = pl.BlockSpec(memory_space=SMEM)
    in_any = pl.BlockSpec(memory_space=pl.ANY)

    def turn(value, axis, size, by):
        return lax.ppermute(value, axis, [(i, (i + by) % size) for i in range(size)])

    sums = pl.pallas_call(
        sum_factors,
        out_shape=(jax.ShapeDtypeStruct((held_rows, width), F32),)
        + (jax.ShapeDtypeStruct((held_rows, width), BF),) * (ny - 1),
        in_specs=[in_any] * 4,
        out_specs=(in_any,) * ny,
        scratch_shapes=[
            VMEM((slots, rank, width), BF),
            VMEM((targets * panels, rank, width), F32),
            VMEM((ny - 1, held_rows, width), BF),
            SMEM((slots,), jnp.int32),
            SMEM((slots,), jnp.int32),
            SMEM((1,), jnp.int32),
            pltpu.SemaphoreType.DMA((5 + ny + mine * panels,)),
            pltpu.SemaphoreType.DMA((3,)),
        ],
        compiler_params=params(56),
        cost_estimate=pl.CostEstimate(flops=10**7, bytes_accessed=7 * 10**6, transcendentals=0),
        name="sum_factors",
    )(entry_panel[:, 0], entry_target[:, 0], entry_count[0], factors)
    held = [sums[0].astype(BF)] + [turn(sums[s], "y", ny, s) for s in range(1, ny)]

    own, _ = lax.optimization_barrier((panel_shared.reshape(rows, LANES), sums))
    pair = jnp.stack([own, turn(own, "core", nc, 1)])
    pieces = [pair] + [turn(pair, "x", nx, s) for s in range(1, nx)]
    columns = jnp.stack(
        [((x + nx - s) % nx) * nc + k for s in range(nx) for k in (c, (c + 1) % nc)]
    ).astype(jnp.int32)
    mine_all, found = pl.pallas_call(
        project,
        out_shape=(
            jax.ShapeDtypeStruct((rows + TAIL, width), F32),
            jax.ShapeDtypeStruct((ny, own_rows, rows), BF),
        ),
        in_specs=[in_smem] + [in_vmem] * (nx + 2),
        out_specs=(in_vmem,) * 2,
        scratch_shapes=[VMEM((rows + TAIL, width), BF)],
        compiler_params=params(60),
        name="project",
    )(columns, *pieces, probes.reshape(targets * rank, width), coupling)
    coefficients = lax.all_to_all(found, "y", 0, 0, tiled=True)
    mine_all = mine_all.astype(BF)

    cut = width // nz
    sketch = pl.pallas_call(
        first_pass,
        out_shape=jax.ShapeDtypeStruct((nz, own_rows, cut), BF),
        in_specs=[in_vmem] * (ny + 1),
        out_specs=in_vmem,
        compiler_params=params(20),
        name="first_pass",
    )(*held, coefficients)
    mine_all, sketch = lax.optimization_barrier((mine_all, sketch))
    near = [turn(mine_all, "y", ny, s) for s in (1, ny - 1)]
    parts = lax.all_to_all(sketch, "z", 0, 0, tiled=True)
    parts, near = lax.optimization_barrier((parts, near))
    far = [turn(near[0][:RELAY], "y", ny, 1), turn(near[1][RELAY:], "y", ny, ny - 1)]
    all_shared = [mine_all, near[0], *far, near[1]]
    copies = pl.pallas_call(
        add_up,
        out_shape=jax.ShapeDtypeStruct((nz, own_rows, cut), BF),
        in_specs=[in_vmem],
        out_specs=in_vmem,
        compiler_params=params(8),
        name="add_up",
    )(parts)
    sketches = lax.all_to_all(copies, "z", 0, 0, tiled=True)

    keep = width // (ny * nz)
    rows_part, *sent = pl.pallas_call(
        second_pass,
        out_shape=(jax.ShapeDtypeStruct((width, own_rows), BF),)
        + (pltpu.HBM((rank + keep, own_rows), F32),) * ny,
        in_specs=[in_smem] + [in_vmem] * 10,
        out_specs=(in_vmem,) + (pl.BlockSpec(memory_space=pltpu.HBM),) * ny,
        scratch_shapes=[
            VMEM((cut, own_rows), F32),
            VMEM((ny, rank + keep, own_rows), F32),
            pltpu.SemaphoreType.DMA((ny,)),
        ],
        compiler_params=params(20),
        name="second_pass",
    )(place, sketches, *held, *all_shared)
    row_parts = lax.all_to_all(rows_part.reshape(ny * nz, keep, own_rows), ("z", "y"), 0, 0, tiled=True)
    received = [pltpu.with_memory_space_constraint(sent[0], pltpu.HBM)] + [turn(sent[s], "y", ny, s) for s in range(1, ny)]
    out = jax.ShapeDtypeStruct((targets, keep, rank), F32)
    left_out, right_out = pl.pallas_call(
        finish,
        out_shape=(out, out),
        in_specs=[in_smem, in_vmem, pl.BlockSpec(memory_space=pltpu.HBM)] + [in_vmem] * (ny - 1),
        out_specs=(in_vmem, in_vmem),
        scratch_shapes=[VMEM((rank + keep, own_rows), F32), pltpu.SemaphoreType.DMA],
        compiler_params=params(8),
        name="finish",
    )(place, row_parts, *received)
    return left_out.transpose(0, 2, 1), right_out.transpose(0, 2, 1)


def solution(mesh):
    wide, narrow = mesh.devices.shape
    sizes = (4, wide // 4, narrow // 2, 2)
    axes = ("y", "z", "x", "core")
    finer = Mesh(mesh.devices.reshape(sizes), axes)
    split, owner = ("y", "z"), ("x", "core")
    placed = (
        P(split, owner, None, None),
        P(split, owner),
        P(split, owner),
        P(owner, split),
        P(split, None, owner),
        P(split, None, None),
        P(owner, None, None),
    )
    return jax.shard_map(
        functools.partial(shards, sizes),
        mesh=finer,
        in_specs=placed,
        out_specs=(P(owner, None, split), P(owner, None, split)),
        check_vma=False,
    )
```

```python
import functools
import math

import jax
import jax.numpy as jnp
from jax import lax
from jax.experimental import pallas as pl
from jax.experimental.pallas import tpu as pltpu
from jax.sharding import Mesh
from jax.sharding import PartitionSpec as P

BF = jnp.bfloat16
F32 = jnp.float32
HIGHEST = lax.Precision.HIGHEST
NT = (((1,), (1,)), ((), ()))
TN = (((0,), (0,)), ((), ()))
SMEM = pltpu.SMEM
VMEM = pltpu.VMEM
LANES = 128
BLOCK = 8
TAIL = 16
RELAY = 80


def params(mib):
    return pltpu.CompilerParams(vmem_limit_bytes=mib * 1024 * 1024)


def split_bf(x, parts):
    out = []
    for _ in range(parts):
        part = x.astype(BF)
        out.append(part)
        x = x - part.astype(F32)
    return out


def pack_rows(block):
    return jnp.concatenate([block[q * TAIL : (q + 1) * TAIL] for q in range(block.shape[0] // TAIL)], axis=1)


def unpack_rows(block):
    return jnp.concatenate([block[:, q * LANES : (q + 1) * LANES] for q in range(block.shape[1] // LANES)], axis=0)


def sum_factors(panel, target, count, factors, *refs):
    out, (loaded, acc, kept, panel_at, target_at, count_at, sems, small) = refs[:-8], refs[-8:]
    slots, rank, _ = loaded.shape
    pairs = acc.shape[0]
    panels = pairs // 8
    chunk = slots // 6
    indices = [
        pltpu.make_async_copy(source, to, small.at[i])
        for i, (source, to) in enumerate(((panel, panel_at), (target, target_at), (count, count_at)))
    ]
    for copy in indices:
        copy.start()
    loads = [
        pltpu.make_async_copy(factors.at[pl.ds(i * chunk, chunk)], loaded.at[pl.ds(i * chunk, chunk)], sems.at[i])
        for i in range(slots // chunk)
    ]
    for copy in loads:
        copy.start()

    def clear(i, _):
        acc[i] = jnp.zeros(acc.shape[1:], F32)
        return 0

    lax.fori_loop(0, pairs, clear, 0)
    for copy in indices:
        copy.wait()
    live = count_at[0]

    def add(e, _):
        pair = target_at[e] * panels + panel_at[e]
        acc[pair] += loaded[e].astype(F32)
        return 0

    for i, copy in enumerate(loads):
        copy.wait()
        lax.fori_loop(i * chunk, jnp.minimum(live, (i + 1) * chunk), add, 0)
    groups = len(out)
    each = pairs // groups
    here = lax.axis_index("y")
    stores = [pltpu.make_async_copy(kept.at[s - 1], out[s], sems.at[5 + s]) for s in range(1, groups)]
    direct = [
        pltpu.make_async_copy(acc.at[here * each + i], out[0].at[pl.ds(i * rank, rank)], sems.at[5 + groups + i])
        for i in range(each)
    ]
    for i in range(each):
        direct[i].start()
    for s in range(1, groups):
        owner = lax.rem(here + s, groups)
        for i in range(each):
            kept[s - 1, i * rank : (i + 1) * rank, :] = acc[owner * each + i].astype(BF)
        stores[s - 1].start()
    for copy in direct + stores:
        copy.wait()


def project(columns, *refs):
    pieces, refs = refs[:4], refs[4:]
    probes, coupling, mine, coefficients, shared = refs
    rows = pieces[0].shape[1]
    at = 0
    for piece in pieces:
        for half in range(piece.shape[0]):
            start = pl.multiple_of(columns[at] * LANES, LANES)
            shared[0:rows, pl.ds(start, LANES)] = piece[half]
            at += 1
    rank = coupling.shape[1]
    zero = jnp.zeros((rank, rank), F32)
    first, second = coupling[0], coupling[1]
    diagonal = jnp.concatenate(
        [jnp.concatenate([first, zero], axis=1), jnp.concatenate([zero, second], axis=1)], axis=0
    )
    projected = lax.dot_general(probes[...], shared[0:rows, :], NT, preferred_element_type=F32)
    found = lax.dot_general(projected, diagonal, NT, precision=HIGHEST, preferred_element_type=F32).astype(BF)
    each = coefficients.shape[1]
    for g in range(coefficients.shape[0]):
        coefficients[g] = found[g * each : (g + 1) * each]
    high, low = split_bf(jnp.concatenate([first, second], axis=1), 2)
    shared[rows : rows + TAIL, :] = jnp.concatenate([pack_rows(high), pack_rows(low)], axis=1)
    mine[...] = shared[...].astype(F32)


def first_pass(*refs):
    held, (coefficients, out) = refs[:-2], refs[-2:]
    groups = len(held)
    here = lax.axis_index("y")
    rows, width = held[0].shape
    targets = rows // LANES
    rank = out.shape[1] // targets
    cut = out.shape[2]
    totals = [jnp.zeros((rank, width), F32) for _ in range(targets)]
    for s in range(groups):
        source = lax.rem(here + groups - s, groups)
        for t in range(targets):
            totals[t] = totals[t] + jnp.dot(
                coefficients[source, t * rank : (t + 1) * rank, :],
                held[s][t * LANES : (t + 1) * LANES, :],
                preferred_element_type=F32,
            )
    for t in range(targets):
        for z in range(out.shape[0]):
            out[z, t * rank : (t + 1) * rank, :] = totals[t][:, z * cut : (z + 1) * cut].astype(BF)


def add_up(parts, above, below, out, first, second, sems):
    moves = [
        pltpu.make_async_copy(above.at[0:RELAY, :], first, sems.at[0]),
        pltpu.make_async_copy(below.at[RELAY:, :], second, sems.at[1]),
    ]
    for copy in moves:
        copy.start()
    total = parts[0].astype(F32)
    for z in range(1, parts.shape[0]):
        total = total + parts[z].astype(F32)
    for z in range(out.shape[0]):
        out[z] = total.astype(out.dtype)
    for copy in moves:
        copy.wait()


def inverse_factors(grams):
    rank = grams[0].shape[0]
    row_at = lax.broadcasted_iota(jnp.int32, (rank, 2 * rank), 0)
    lane_at = lax.broadcasted_iota(jnp.int32, (rank, 2 * rank), 1)
    eye = (row_at + rank == lane_at).astype(F32)
    tables = [jnp.concatenate([g, jnp.zeros((rank, rank), F32)], axis=1) + eye for g in grams]
    for first in range(0, rank, BLOCK):
        top = (first // 8) * 8
        at = first - top
        for i, table in enumerate(tables):
            lower = table[top:, :]
            columns = [
                jnp.broadcast_to(lower[:, first + j : first + j + 1], lower.shape) for j in range(BLOCK)
            ]
            pivots = [lower[at + j : at + j + 1, :] for j in range(BLOCK)]
            for j in range(BLOCK):
                own = columns[j][at + j : at + j + 1, :]
                share = jnp.where(row_at[top:, :] > first + j, columns[j] * (1.0 / own), 0.0)
                for k in range(j + 1, BLOCK):
                    columns[k] = columns[k] - share * columns[j][at + k : at + k + 1, :]
                    pivots[k] = pivots[k] - share[at + k : at + k + 1, :] * pivots[j]
                lower = lower - share * pivots[j]
            tables[i] = lower if top == 0 else jnp.concatenate([table[:top], lower], axis=0)
    diagonal = row_at == lane_at
    return [
        (table * lax.rsqrt(jnp.sum(jnp.where(diagonal, table, 0.0), axis=1, keepdims=True)))[:, rank:]
        for table in tables
    ]


def second_pass(place, sketches, *refs):
    held, refs = refs[:4], refs[4:]
    groups = len(held)
    out, sent, (turned, kept, sems) = refs[5], refs[6:-3], refs[-3:]
    cuts, rows, cut = sketches.shape
    width = held[0].shape[1]
    targets = held[0].shape[0] // LANES
    rank = rows // targets
    whole = [
        jnp.concatenate([sketches[z, t * rank : (t + 1) * rank, :] for z in range(cuts)], axis=1)
        for t in range(targets)
    ]
    grams = [lax.dot_general(s, s, NT, preferred_element_type=F32) for s in whole]
    inverses = jnp.concatenate(inverse_factors(grams), axis=1)
    panels = [refs[0][...], refs[1][...], jnp.concatenate([refs[2][...], refs[3][...]], axis=0), refs[4][...]]
    half = width // 2
    own = sent[0].shape[0] - rank
    total = jnp.zeros((rows, width), F32)
    for s in range(groups):
        summed = jnp.concatenate(
            [
                lax.dot_general(
                    held[s][t * LANES : (t + 1) * LANES, :], whole[t], NT, preferred_element_type=F32
                )
                for t in range(targets)
            ],
            axis=1,
        )
        coupling = unpack_rows(panels[s][LANES:, :half]).astype(F32) + unpack_rows(panels[s][LANES:, half:]).astype(F32)
        middle = jnp.concatenate(
            [
                lax.dot_general(
                    coupling[:, d * rank : (d + 1) * rank],
                    summed[d * rank : (d + 1) * rank, :],
                    TN,
                    precision=HIGHEST,
                    preferred_element_type=F32,
                )
                for d in range(LANES // rank)
            ],
            axis=0,
        ).T
        for part in split_bf(middle, 2):
            total = total + jnp.dot(part, panels[s][0:LANES], preferred_element_type=F32)
    for c in range(width // LANES):
        block = total[:, c * LANES : (c + 1) * LANES].T.astype(out.dtype)
        for k in range(LANES // own):
            first = c * (LANES // own) + k
            to = (first % cuts) * groups + first // cuts
            out[to * own : (to + 1) * own, :] = block[k * own : (k + 1) * own]
    for s in range(groups):
        owner = lax.rem(place[0] + s, groups)
        start = owner * (width // groups) + place[1] * own
        piece = start // cut
        turned[...] = sketches[piece].astype(F32).T
        kept[s, 0:rank, :] = inverses
        kept[s, rank : rank + own, :] = turned[pl.ds(pl.multiple_of(start - piece * cut, 32), own), :]
    copies = [pltpu.make_async_copy(kept.at[s], sent[s], sems.at[s]) for s in range(groups)]
    for copy in copies:
        copy.start()
    for copy in copies:
        copy.wait()


def finish(place, parts, own_far, *refs):
    received, (left, right, own_near, sem) = refs[:-4], refs[-4:]
    copy = pltpu.make_async_copy(own_far, own_near, sem)
    copy.start()
    received = [own_near, *received]
    owners = len(received)
    groups = parts.shape[0] // owners
    targets = left.shape[0] // owners
    own, rank = left.shape[1], left.shape[2]
    root = math.sqrt(1024)
    for s in [*range(1, owners), 0]:
        if s == 0:
            copy.wait()
        owner = lax.rem(place[0] + owners - s, owners)
        total = parts[owner].astype(F32)
        for z in range(1, groups):
            total = total + parts[z * owners + owner].astype(F32)
        both = jnp.concatenate([received[s][rank : rank + own, :] * root, total / root], axis=0)
        for t in range(targets):
            found = lax.dot_general(
                both[:, t * rank : (t + 1) * rank],
                received[s][0:rank, t * rank : (t + 1) * rank],
                NT,
                precision=HIGHEST,
                preferred_element_type=F32,
            )
            left[owner * targets + t] = found[0:own]
            right[owner * targets + t] = found[own : 2 * own]


def shards(sizes, entry_factor, entry_panel, entry_target, entry_count, panel_shared, coupling, probes):
    ny, nz, nx, nc = sizes
    y, z = lax.axis_index("y"), lax.axis_index("z")
    x, c = lax.axis_index("x"), lax.axis_index("core")
    place = jnp.stack([y, z, c]).astype(jnp.int32)
    factors = entry_factor[:, 0]
    slots, rank, width = factors.shape
    panels = panel_shared.shape[0]
    targets = probes.shape[0]
    rows = panels * rank
    mine = targets // ny
    own_rows = mine * rank
    held_rows = mine * panels * rank
    in_vmem = pl.BlockSpec(memory_space=VMEM)
    in_smem = pl.BlockSpec(memory_space=SMEM)
    in_any = pl.BlockSpec(memory_space=pl.ANY)

    def turn(value, axis, size, by):
        return lax.ppermute(value, axis, [(i, (i + by) % size) for i in range(size)])

    sums = pl.pallas_call(
        sum_factors,
        out_shape=(jax.ShapeDtypeStruct((held_rows, width), F32),)
        + (jax.ShapeDtypeStruct((held_rows, width), BF),) * (ny - 1),
        in_specs=[in_any] * 4,
        out_specs=(in_any,) * ny,
        scratch_shapes=[
            VMEM((slots, rank, width), BF),
            VMEM((targets * panels, rank, width), F32),
            VMEM((ny - 1, held_rows, width), BF),
            SMEM((slots,), jnp.int32),
            SMEM((slots,), jnp.int32),
            SMEM((1,), jnp.int32),
            pltpu.SemaphoreType.DMA((5 + ny + mine * panels,)),
            pltpu.SemaphoreType.DMA((3,)),
        ],
        compiler_params=params(56),
        cost_estimate=pl.CostEstimate(flops=10**7, bytes_accessed=7 * 10**6, transcendentals=0),
        name="sum_factors",
    )(entry_panel[:, 0], entry_target[:, 0], entry_count[0], factors)
    held = [sums[0].astype(BF)] + [turn(sums[s], "y", ny, s) for s in range(1, ny)]

    own, _ = lax.optimization_barrier((panel_shared.reshape(rows, LANES), sums))
    pair = jnp.stack([own, turn(own, "core", nc, 1)])
    pieces = [pair] + [turn(pair, "x", nx, s) for s in range(1, nx)]
    columns = jnp.stack(
        [((x + nx - s) % nx) * nc + k for s in range(nx) for k in (c, (c + 1) % nc)]
    ).astype(jnp.int32)
    mine_all, found = pl.pallas_call(
        project,
        out_shape=(
            jax.ShapeDtypeStruct((rows + TAIL, width), F32),
            jax.ShapeDtypeStruct((ny, own_rows, rows), BF),
        ),
        in_specs=[in_smem] + [in_vmem] * (nx + 2),
        out_specs=(in_vmem,) * 2,
        scratch_shapes=[VMEM((rows + TAIL, width), BF)],
        compiler_params=params(60),
        name="project",
    )(columns, *pieces, probes.reshape(targets * rank, width), coupling)
    coefficients = lax.all_to_all(found, "y", 0, 0, tiled=True)
    mine_all = mine_all.astype(BF)

    cut = width // nz
    sketch = pl.pallas_call(
        first_pass,
        out_shape=jax.ShapeDtypeStruct((nz, own_rows, cut), BF),
        in_specs=[in_vmem] * (ny + 1),
        out_specs=in_vmem,
        compiler_params=params(20),
        name="first_pass",
    )(*held, coefficients)
    mine_all, sketch = lax.optimization_barrier((mine_all, sketch))
    near = [turn(mine_all, "y", ny, s) for s in (1, ny - 1)]
    parts = lax.all_to_all(sketch, "z", 0, 0, tiled=True)
    parts, near = lax.optimization_barrier((parts, near))
    copies, above, below = pl.pallas_call(
        add_up,
        out_shape=(
            jax.ShapeDtypeStruct((nz, own_rows, cut), BF),
            pltpu.HBM((RELAY, width), BF),
            pltpu.HBM((rows + TAIL - RELAY, width), BF),
        ),
        in_specs=[in_vmem] * 3,
        out_specs=(in_vmem,) + (pl.BlockSpec(memory_space=pltpu.HBM),) * 2,
        scratch_shapes=[pltpu.SemaphoreType.DMA((2,))],
        compiler_params=params(8),
        name="add_up",
    )(parts, *near)
    far = [turn(above, "y", ny, 1), turn(below, "y", ny, ny - 1)]
    all_shared = [mine_all, near[0], *far, near[1]]
    sketches = lax.all_to_all(copies, "z", 0, 0, tiled=True)

    keep = width // (ny * nz)
    rows_part, *sent = pl.pallas_call(
        second_pass,
        out_shape=(jax.ShapeDtypeStruct((width, own_rows), BF),)
        + (pltpu.HBM((rank + keep, own_rows), F32),) * ny,
        in_specs=[in_smem] + [in_vmem] * 10,
        out_specs=(in_vmem,) + (pl.BlockSpec(memory_space=pltpu.HBM),) * ny,
        scratch_shapes=[
            VMEM((cut, own_rows), F32),
            VMEM((ny, rank + keep, own_rows), F32),
            pltpu.SemaphoreType.DMA((ny,)),
        ],
        compiler_params=params(20),
        name="second_pass",
    )(place, sketches, *held, *all_shared)
    row_parts = lax.all_to_all(rows_part.reshape(ny * nz, keep, own_rows), ("z", "y"), 0, 0, tiled=True)
    received = [pltpu.with_memory_space_constraint(sent[0], pltpu.HBM)] + [turn(sent[s], "y", ny, s) for s in range(1, ny)]
    out = jax.ShapeDtypeStruct((targets, keep, rank), F32)
    left_out, right_out = pl.pallas_call(
        finish,
        out_shape=(out, out),
        in_specs=[in_smem, in_vmem, pl.BlockSpec(memory_space=pltpu.HBM)] + [in_vmem] * (ny - 1),
        out_specs=(in_vmem, in_vmem),
        scratch_shapes=[VMEM((rank + keep, own_rows), F32), pltpu.SemaphoreType.DMA],
        compiler_params=params(8),
        name="finish",
    )(place, row_parts, *received)
    return left_out.transpose(0, 2, 1), right_out.transpose(0, 2, 1)


def solution(mesh):
    wide, narrow = mesh.devices.shape
    sizes = (4, wide // 4, narrow // 2, 2)
    axes = ("y", "z", "x", "core")
    finer = Mesh(mesh.devices.reshape(sizes), axes)
    split, owner = ("y", "z"), ("x", "core")
    placed = (
        P(split, owner, None, None),
        P(split, owner),
        P(split, owner),
        P(owner, split),
        P(split, None, owner),
        P(split, None, None),
        P(owner, None, None),
    )
    return jax.shard_map(
        functools.partial(shards, sizes),
        mesh=finer,
        in_specs=placed,
        out_specs=(P(owner, None, split), P(owner, None, split)),
        check_vma=False,
    )
```
